32 devices in a mesh: leaf: 32 (over z, y, x, core).
Axes of the slice: x: 2, y: 2, z: 4, core: 2. Of those that a mesh axis runs over, the one named last changes fastest.
Arguments:
- points: bfloat16 [64, 131072], P(None, 'leaf'), may hold values from -3 to 7
- weights: bfloat16 [32, 131072], P(None, 'leaf'), may hold values from -6 to 6
- skel_index: int32 [16384], P('leaf'), may hold values from 0 to 4095, as said below
- assign: int32 [131072], P('leaf'), may hold values from 0 to 511
- near_leaf: int32 [256, 12], replicated, may hold values from 0 to 255, as said below
- near_count: int32 [256], replicated, may hold values from 6 to 12
Outputs:
- near_field: float32 [32, 131072], P(None, 'leaf')
- far_field: float32 [32, 131072], P(None, 'leaf')
The draws below stay inside these ranges and needn't reach their ends.
Inputs may be any that keep to these rules, and one draw needn't show every extreme that they name: `skel_index`: each device's 512 entries are distinct. `near_leaf`: leaf id g belongs to device g // 8. For each device r, its 96 entries read leaf by leaf and taken in runs of 32 - 1 (the last run may be shorter) name leaves of devices other than r, of distinct devices within a run; so a device reads at most 4 blocks from any one device, and this is reached.
All inputs are finite; a program needn't handle non-finite values.
Results may differ from the reference program's by a relative error of at most 0.0088.
Values may be sent and summed in bfloat16 or wider, within the bound.
A program may use at most 128 MiB of HBM per device.

```python
import math
import jax
import jax.numpy as jnp
from jax import lax

D = 64
RHS = 32
LEAF = 512
SKEL = 512
NEAR = 12
LEAVES_DEV = 8
LEAVES = 256
POINTS = 131072
SKEL_ALL = 16384
LEVELS = 5
N_LEAF = 32


def draw_points(key, part):
    latent_key, noise_key = jax.random.split(jax.random.fold_in(key, 31))
    latent = jnp.clip(jax.random.normal(latent_key, (4, POINTS), jnp.float32), -3.5, 3.5)
    noise = jnp.clip(0.5 * jax.random.normal(noise_key, (D, POINTS), jnp.float32), -1.5, 1.5)
    centre = 2.0
    spread = jnp.tile(latent, (D // 4, 1))
    return (centre + spread + noise).astype(jnp.bfloat16)


def draw_skel_index(key, part):
    device_count = SKEL_ALL // SKEL
    p_dev = LEAVES_DEV * LEAF

    def one_device(dev_key):
        first_key, second_key = jax.random.split(dev_key)
        inner = 1 + jax.random.permutation(first_key, p_dev - 2)[:SKEL - 2]
        whole = jnp.concatenate([jnp.array([0, p_dev - 1], jnp.int32), inner.astype(jnp.int32)])
        return whole[jax.random.permutation(second_key, SKEL)]
    return jax.vmap(one_device)(jax.random.split(jax.random.fold_in(key, 5), device_count)).reshape(-1).astype(jnp.int32)


def draw_near_leaf(key, part):
    device_count = LEAVES // LEAVES_DEV
    slot_count = LEAVES_DEV * NEAR
    perm_key, local_key = jax.random.split(jax.random.fold_in(key, 11))

    def one_reader(reader_key, reader):
        offsets = (1 + jax.random.permutation(reader_key, device_count - 1)).astype(jnp.int32)
        spot = jnp.argmax((offsets == device_count - 1).astype(jnp.int32))
        forced = offsets.at[spot].set(offsets[0]).at[0].set(device_count - 1)
        offsets = jnp.where(reader < 2, forced, offsets)
        slot_pos = jnp.arange(slot_count, dtype=jnp.int32) % (device_count - 1)
        return (reader + offsets[slot_pos]) % device_count
    owners = jax.vmap(one_reader)(jax.random.split(perm_key, device_count), jnp.arange(device_count, dtype=jnp.int32))
    local_ids = jax.random.randint(local_key, (device_count, slot_count), 0, LEAVES_DEV).astype(jnp.int32)
    local_ids = local_ids.at[0, 0].set(LEAVES_DEV - 1).at[1, 0].set(0)
    return (owners * LEAVES_DEV + local_ids).reshape(LEAVES, NEAR).astype(jnp.int32)


def draw_near_count(key, part):
    device_count = LEAVES // LEAVES_DEV
    heavy_key, light_key = jax.random.split(jax.random.fold_in(key, 23))
    heavy = jax.random.randint(heavy_key, (device_count,), 0, 4) == 0
    heavy = heavy.at[0].set(True).at[1].set(False)
    light = jax.random.randint(light_key, (device_count, LEAVES_DEV), NEAR // 2, NEAR + 1).astype(jnp.int32)
    light = light.at[1, 0].set(NEAR // 2)
    counts = jnp.where(heavy[:, None], NEAR, light)
    return counts.reshape(LEAVES).astype(jnp.int32)


def plant(values, stream_key, least, high):
    extent = values.shape
    index_at = [jax.random.randint(jax.random.fold_in(stream_key, axis), (), 0, extent[axis]) for axis in range(len(extent))]
    values = values.at[tuple(index_at)].set(least)
    longest = extent.index(max(extent))
    index_at[longest] = (index_at[longest] + 1) % extent[longest]
    return values.at[tuple(index_at)].set(high)


def block_levels(stream_key, dims, cuts, low, largest):
    gain = 1.0
    for axis_at, blocks in cuts:
        heights = jax.random.uniform(jax.random.fold_in(jax.random.fold_in(stream_key, 6), axis_at), (blocks,), jnp.float32, low / len(cuts), largest / len(cuts))
        gain = gain * jnp.repeat(jnp.exp(heights), dims[axis_at] // blocks).reshape((-1,) + (1,) * (len(dims) - 1 - axis_at))
    return gain


def gaussian(rng, dims, scale, bound, shards=(), kind=jnp.bfloat16):
    drawn = jax.random.normal(rng, dims, jnp.float32) * scale
    if len(shards) > 0:
        drawn = block_levels(rng, dims, shards, -0.22, 0.18) * drawn
    return jnp.clip(drawn, min=-bound, max=bound).astype(kind)


def setup_inputs(seed: int = 0) -> dict:
    key_of = jax.random.split(jax.random.key(seed), 7)
    points = draw_points(jax.random.fold_in(key_of[6], 71), 0)
    weights = gaussian(key_of[1], (RHS, POINTS), 1.0, 6.0, ((1, 32),))
    skel_index = draw_skel_index(jax.random.fold_in(key_of[6], 71), 0)
    assign = plant(jax.random.randint(key_of[3], (POINTS,), 0, SKEL), jax.random.fold_in(key_of[3], 1), 0, SKEL - 1).astype(jnp.int32)
    near_leaf = draw_near_leaf(jax.random.fold_in(key_of[6], 71), 0)
    near_count = draw_near_count(jax.random.fold_in(key_of[6], 71), 0)
    return {"points": points, "weights": weights, "skel_index": skel_index, "assign": assign, "near_leaf": near_leaf, "near_count": near_count}


def kernel_apply(targets, sources, source_w):
    inner_prod = lax.dot_general(sources, targets, (((0,), (0,)), ((), ())), preferred_element_type=jnp.float32)
    target_sq = lax.optimization_barrier(jnp.sum(jnp.square(targets.astype(jnp.float32)), axis=0))
    source_sq = lax.optimization_barrier(jnp.sum(jnp.square(sources.astype(jnp.float32)), axis=0))
    sq_dist = source_sq[:, None] + target_sq[None, :] - 2.0 * inner_prod
    kernel_tile = jnp.exp(sq_dist * (-1.0 / D)).astype(jnp.bfloat16)
    return jnp.dot(source_w, kernel_tile, preferred_element_type=jnp.float32)

def fold_child(node_stack):
    half_width = node_stack.shape[-1] // 2
    node_weights = node_stack[..., D:, :half_width].astype(jnp.float32) + node_stack[..., D:, half_width:].astype(jnp.float32)
    return jnp.concatenate([node_stack[..., :D, :half_width], node_weights.astype(jnp.bfloat16)], axis=-2)

def merge_pair(lower_child, upper_child):
    return jnp.concatenate([fold_child(lower_child), fold_child(upper_child)], axis=-1)

def reference(points, weights, skel_index, assign, near_leaf, near_count):
    p_dev = LEAVES_DEV * LEAF
    stacked = jnp.concatenate([points, weights], axis=0)
    leaf_blocks = stacked.reshape(D + RHS, LEAVES, LEAF).transpose(1, 0, 2)

    def near_one(packed):
        leaf_ids, used, own_block = packed
        neighbours = leaf_blocks[leaf_ids]

        def one_term(source_block):
            return kernel_apply(own_block[:D], source_block[:D], source_block[D:])
        terms = jax.vmap(one_term)(neighbours)
        live_slot = (jnp.arange(NEAR, dtype=jnp.int32) < used).astype(jnp.float32)
        own_term = kernel_apply(own_block[:D], own_block[:D], own_block[D:])
        return own_term + lax.optimization_barrier(jnp.sum(terms * live_slot[:, None, None], axis=0))
    near_sum = lax.map(near_one, (near_leaf, near_count, leaf_blocks))
    near_field = near_sum.transpose(1, 0, 2).reshape(RHS, POINTS) * (4.0 / math.sqrt(LEAF * (NEAR + 1)))
    device_blocks = stacked.reshape(D + RHS, N_LEAF, p_dev).transpose(1, 0, 2)

    def base_one(packed):
        device_block, chosen, owner_skel = packed
        skel_points = device_block[:D][:, chosen]
        summed = jax.ops.segment_sum(device_block[D:].astype(jnp.float32).T, owner_skel, SKEL).T
        return jnp.concatenate([skel_points, summed.astype(jnp.bfloat16)], axis=0)
    node_stack = lax.map(base_one, (device_blocks, skel_index.reshape(N_LEAF, SKEL), assign.reshape(N_LEAF, p_dev)))
    device_ids = jnp.arange(N_LEAF, dtype=jnp.int32)
    far_sum = jnp.zeros((N_LEAF, RHS, p_dev), jnp.float32)

    def far_one(packed):
        device_block, partner = packed
        return kernel_apply(device_block[:D], partner[:D], partner[D:])
    for depth_bit in range(LEVELS):
        partners = node_stack[device_ids >> depth_bit ^ 1]
        far_sum = far_sum + lax.map(far_one, (device_blocks, partners))
        if depth_bit + 1 < LEVELS:
            node_stack = merge_pair(node_stack[0::2], node_stack[1::2])
    far_field = far_sum.transpose(1, 0, 2).reshape(RHS, POINTS) * (4.0 / math.sqrt(POINTS))
    return (near_field, far_field)
```

```python
import functools
import math

import jax
import jax.numpy as jnp
from jax import lax
from jax.experimental import pallas as pl
from jax.experimental.pallas import tpu as pltpu
from jax.sharding import PartitionSpec as P

D = 64
RHS = 32
LEAF = 512
SKEL = 512
NEAR = 12
ROWS = D + RHS
DEPTH = 256
SCALE2 = 1.0 / (D * math.log(2.0))
SLOTS = 4


def three_parts(x):
    high = x.astype(jnp.bfloat16).astype(jnp.float32)
    rest = x - high
    mid = rest.astype(jnp.bfloat16).astype(jnp.float32)
    low = (rest - mid).astype(jnp.bfloat16).astype(jnp.float32)
    return high, mid, low


def neg_norm_parts(points32):
    norm = jnp.sum(points32 * points32, axis=0, keepdims=True) * (-SCALE2)
    return three_parts(norm)


def tail_rows(parts, first, ones_first, rows):
    row = lax.broadcasted_iota(jnp.int32, (rows, parts[0].shape[1]), 0)
    tail = jnp.where((row >= ones_first) & (row < ones_first + 3), 1.0, 0.0)
    for step, part in enumerate(parts):
        tail = jnp.where(row == first + step, part, tail)
    return tail


def target_side(points):
    points32 = points.astype(jnp.float32)
    parts = three_parts(points32 * (2.0 * SCALE2))
    tail = tail_rows(neg_norm_parts(points32), 3, 0, DEPTH - 3 * D)
    return jnp.concatenate([*parts, tail], axis=0).T.astype(jnp.bfloat16)


def source_side(points):
    tail = tail_rows(neg_norm_parts(points.astype(jnp.float32)), 0, 3, DEPTH - 3 * D)
    return jnp.concatenate([points, points, points, tail.astype(jnp.bfloat16)], axis=0)


def tile_term(target, points, weights):
    exponent = jnp.dot(target, source_side(points), preferred_element_type=jnp.float32)
    tile = jnp.exp2(exponent).astype(jnp.bfloat16)
    return lax.dot_general(
        tile, weights, (((1,), (1,)), ((), ())), preferred_element_type=jnp.float32
    )


def local_kernel(depth_count, far_scale, points_ref, weights_ref, nodes_ref, self_ref, far_ref):
    points = points_ref[...]
    target = target_side(points)
    self_ref[...] = tile_term(target, points, weights_ref[...]).T
    total = jnp.zeros((LEAF, RHS), jnp.float32)
    for level in range(depth_count):
        total = total + tile_term(target, nodes_ref[level, :D, :], nodes_ref[level, D:, :])
    far_ref[...] = total.T * far_scale


def near_kernel(leaves_dev, near_scale, owner_ref, place_ref, start_ref, points_ref, self_ref,
                blocks_ref, out_ref, held, sems):
    total_items = start_ref[leaves_dev]

    def fetch(item):
        slot = lax.rem(item, SLOTS)
        column = pl.multiple_of(place_ref[item] * LEAF, LEAF)
        return pltpu.make_async_copy(
            blocks_ref.at[owner_ref[item], :, pl.ds(column, LEAF)], held.at[slot], sems.at[slot]
        )

    for ahead in range(SLOTS - 1):
        @pl.when(ahead < total_items)
        def _():
            fetch(ahead).start()

    def leaf_step(leaf, carry):
        columns = pl.ds(pl.multiple_of(leaf * LEAF, LEAF), LEAF)
        target = target_side(points_ref[:, columns])

        def item_step(item, running):
            @pl.when(item + SLOTS - 1 < total_items)
            def _():
                fetch(item + SLOTS - 1).start()
            fetch(item).wait()
            slot = lax.rem(item, SLOTS)
            return running + tile_term(target, held[slot, :D, :], held[slot, D:, :])

        total = lax.fori_loop(
            start_ref[leaf], start_ref[leaf + 1], item_step, jnp.zeros((LEAF, RHS), jnp.float32)
        )
        out_ref[:, columns] = (total.T + self_ref[:, columns]) * near_scale
        return carry

    lax.fori_loop(0, leaves_dev, leaf_step, 0)


def fold_child(nodes):
    half = nodes.shape[-1] // 2
    folded = nodes[..., D:, :half].astype(jnp.float32) + nodes[..., D:, half:].astype(jnp.float32)
    return jnp.concatenate([nodes[..., :D, :half], folded.astype(jnp.bfloat16)], axis=-2)


def sibling_nodes(nodes, my_index, depth_count):
    found = []
    for level in range(depth_count):
        found.append(lax.dynamic_index_in_dim(nodes, (my_index >> level) ^ 1, 0, keepdims=False))
        if level + 1 < depth_count:
            child = fold_child(nodes)
            nodes = jnp.concatenate([child[0::2], child[1::2]], axis=-1)
    return jnp.stack(found)


def per_device(points, weights, skel_index, assign, near_leaf, near_count):
    n_dev = lax.axis_size("leaf")
    my_index = lax.axis_index("leaf")
    depth_count = n_dev.bit_length() - 1
    p_dev = points.shape[1]
    leaves_dev = p_dev // LEAF

    member = (assign[None, :] == jnp.arange(SKEL, dtype=jnp.int32)[:, None]).astype(jnp.bfloat16)
    base_weights = lax.dot_general(
        weights, member, (((1,), (1,)), ((), ())), preferred_element_type=jnp.float32
    )
    base_node = jnp.concatenate([points[:, skel_index], base_weights.astype(jnp.bfloat16)], axis=0)
    stacked = jnp.concatenate([points, weights], axis=0)
    base_node, stacked = lax.optimization_barrier((base_node, stacked))
    nodes = lax.all_gather(base_node, "leaf")
    blocks = lax.all_gather(stacked, "leaf")

    slot_count = leaves_dev * NEAR
    my_leaf = lax.dynamic_slice_in_dim(near_leaf, my_index * leaves_dev, leaves_dev).reshape(-1)
    my_count = lax.dynamic_slice_in_dim(near_count, my_index * leaves_dev, leaves_dev)
    before = jnp.arange(leaves_dev + 1)[:, None] > jnp.arange(leaves_dev)[None, :]
    start = jnp.sum(jnp.where(before, my_count[None, :], 0), axis=1).astype(jnp.int32)
    slot = jnp.arange(slot_count, dtype=jnp.int32)
    live = slot % NEAR < jnp.repeat(my_count, NEAR)
    spot = jnp.where(live, jnp.repeat(start[:-1], NEAR) + slot % NEAR, slot_count)
    chosen = spot[None, :] == slot[:, None]
    item_leaf = jnp.sum(jnp.where(chosen, my_leaf[None, :], 0), axis=1).astype(jnp.int32)

    siblings = sibling_nodes(nodes, my_index, depth_count)
    tile_flops = 2 * LEAF * LEAF * (DEPTH + 256)
    column_block = lambda rows: pl.BlockSpec((rows, LEAF), lambda leaf: (0, leaf))
    self_term, far_field = pl.pallas_call(
        functools.partial(local_kernel, depth_count, 4.0 / math.sqrt(p_dev * n_dev)),
        grid=(leaves_dev,),
        in_specs=[
            column_block(D),
            column_block(RHS),
            pl.BlockSpec((depth_count, ROWS, SKEL), lambda leaf: (0, 0, 0)),
        ],
        out_specs=[column_block(RHS), column_block(RHS)],
        out_shape=[jax.ShapeDtypeStruct((RHS, p_dev), jnp.float32)] * 2,
        compiler_params=pltpu.CompilerParams(vmem_limit_bytes=48 * 2**20),
        cost_estimate=pl.CostEstimate(
            flops=leaves_dev * (depth_count + 1) * tile_flops,
            bytes_accessed=4 * 2**20,
            transcendentals=leaves_dev * (depth_count + 1) * LEAF * LEAF,
        ),
        name="local_and_far",
    )(points, weights, siblings)

    whole = pl.BlockSpec(memory_space=pltpu.VMEM)
    scalars = pl.BlockSpec(memory_space=pltpu.SMEM)
    near_field = pl.pallas_call(
        functools.partial(near_kernel, leaves_dev, 4.0 / math.sqrt(LEAF * (NEAR + 1))),
        in_specs=[scalars, scalars, scalars, whole, whole, pl.BlockSpec(memory_space=pl.ANY)],
        out_specs=whole,
        out_shape=jax.ShapeDtypeStruct((RHS, p_dev), jnp.float32),
        scratch_shapes=[
            pltpu.VMEM((SLOTS, ROWS, LEAF), jnp.bfloat16),
            pltpu.SemaphoreType.DMA((SLOTS,)),
        ],
        compiler_params=pltpu.CompilerParams(vmem_limit_bytes=48 * 2**20),
        cost_estimate=pl.CostEstimate(
            flops=slot_count * tile_flops,
            bytes_accessed=slot_count * ROWS * LEAF * 2,
            transcendentals=slot_count * LEAF * LEAF,
        ),
        name="near_blocks",
    )(item_leaf // leaves_dev, item_leaf % leaves_dev, start, points, self_term, blocks)
    return (near_field, far_field)


def solution(mesh):
    return jax.shard_map(
        per_device,
        mesh=mesh,
        in_specs=(P(None, "leaf"), P(None, "leaf"), P("leaf"), P("leaf"), P(), P()),
        out_specs=(P(None, "leaf"), P(None, "leaf")),
        check_vma=False,
    )
```

```python
import functools
import math

import jax
import jax.numpy as jnp
from jax import lax
from jax.experimental import pallas as pl
from jax.experimental.pallas import tpu as pltpu
from jax.sharding import PartitionSpec as P

D = 64
RHS = 32
LEAF = 512
SKEL = 512
NEAR = 12
ROWS = D + RHS
DEPTH = 256
SCALE2 = 1.0 / (D * math.log(2.0))
SLOTS = 4
FITS = 32 * 2**20


def three_parts(x):
    high = x.astype(jnp.bfloat16).astype(jnp.float32)
    rest = x - high
    mid = rest.astype(jnp.bfloat16).astype(jnp.float32)
    low = (rest - mid).astype(jnp.bfloat16).astype(jnp.float32)
    return high, mid, low


def neg_norm_parts(points32):
    norm = jnp.sum(points32 * points32, axis=0, keepdims=True) * (-SCALE2)
    return three_parts(norm)


def tail_rows(parts, first, ones_first, rows):
    row = lax.broadcasted_iota(jnp.int32, (rows, parts[0].shape[1]), 0)
    tail = jnp.where((row >= ones_first) & (row < ones_first + 3), 1.0, 0.0)
    for step, part in enumerate(parts):
        tail = jnp.where(row == first + step, part, tail)
    return tail


def target_side(points):
    points32 = points.astype(jnp.float32)
    parts = three_parts(points32 * (2.0 * SCALE2))
    tail = tail_rows(neg_norm_parts(points32), 3, 0, DEPTH - 3 * D)
    return jnp.concatenate([*parts, tail], axis=0).T.astype(jnp.bfloat16)


def source_side(points):
    tail = tail_rows(neg_norm_parts(points.astype(jnp.float32)), 0, 3, DEPTH - 3 * D)
    return jnp.concatenate([points, points, points, tail.astype(jnp.bfloat16)], axis=0)


def tile_term(target, points, weights):
    exponent = jnp.dot(target, source_side(points), preferred_element_type=jnp.float32)
    tile = jnp.exp2(exponent).astype(jnp.bfloat16)
    return lax.dot_general(
        tile, weights, (((1,), (1,)), ((), ())), preferred_element_type=jnp.float32
    )


def local_kernel(depth_count, far_scale, points_ref, weights_ref, nodes_ref, self_ref, far_ref):
    points = points_ref[...]
    target = target_side(points)
    self_ref[...] = tile_term(target, points, weights_ref[...]).T
    total = jnp.zeros((LEAF, RHS), jnp.float32)
    for level in range(depth_count):
        total = total + tile_term(target, nodes_ref[level, :D, :], nodes_ref[level, D:, :])
    far_ref[...] = total.T * far_scale


def near_kernel(leaves_dev, near_scale, owner_ref, place_ref, start_ref, points_ref, self_ref,
                blocks_ref, out_ref, held, sems):
    total_items = start_ref[leaves_dev]

    def fetch(item):
        slot = lax.rem(item, SLOTS)
        column = pl.multiple_of(place_ref[item] * LEAF, LEAF)
        return pltpu.make_async_copy(
            blocks_ref.at[owner_ref[item], :, pl.ds(column, LEAF)], held.at[slot], sems.at[slot]
        )

    for ahead in range(SLOTS - 1):
        @pl.when(ahead < total_items)
        def _():
            fetch(ahead).start()

    def leaf_step(leaf, carry):
        columns = pl.ds(pl.multiple_of(leaf * LEAF, LEAF), LEAF)
        target = target_side(points_ref[:, columns])

        def item_step(item, running):
            @pl.when(item + SLOTS - 1 < total_items)
            def _():
                fetch(item + SLOTS - 1).start()
            fetch(item).wait()
            slot = lax.rem(item, SLOTS)
            return running + tile_term(target, held[slot, :D, :], held[slot, D:, :])

        total = lax.fori_loop(
            start_ref[leaf], start_ref[leaf + 1], item_step, jnp.zeros((LEAF, RHS), jnp.float32)
        )
        out_ref[:, columns] = (total.T + self_ref[:, columns]) * near_scale
        return carry

    lax.fori_loop(0, leaves_dev, leaf_step, 0)


def merged(mine, sibling, upper_bit):
    half = SKEL // 2
    parts = []
    for node in (mine, sibling):
        weights = node[D:, :half].astype(jnp.float32) + node[D:, half:].astype(jnp.float32)
        parts.append(
            jnp.concatenate([node[:D, :half].astype(jnp.float32), weights], axis=0)
        )
    lower = jnp.where(upper_bit == 0, parts[0], parts[1])
    upper = jnp.where(upper_bit == 0, parts[1], parts[0])
    return jnp.concatenate([lower, upper], axis=1).astype(jnp.bfloat16)


def fused_kernel(n_dev, caps, near_scale, far_scale, item_ref, spot_ref, leaves_ref, base_ref,
                 near_ref, far_ref, own, beside, below, across, targets, results, mine, sibling,
                 recv, send_x, send_y, send_core, send_up, send_down, node_send, node_recv,
                 local_sem):
    planes = n_dev // 8
    depth_count = n_dev.bit_length() - 1
    leaves_dev = leaves_ref.shape[0]
    half = leaves_dev // 2
    cap = max(caps)
    held = (own, beside, below, across)
    me = lax.axis_index("leaf")
    bits = [(me // 2**level) % 2 for level in range(depth_count)]
    partners = [me + (1 - 2 * bits[level]) * 2**level for level in range(depth_count)]
    core, plane = bits[0], me // 8
    core_dev, x_dev, y_dev = partners[:3]
    up_dev, down_dev = me + 8, me - 8

    barrier = pltpu.get_barrier_semaphore()

    def greet(device):
        pl.semaphore_signal(
            barrier, inc=1, device_id=(device,), device_id_type=pl.DeviceIdType.MESH
        )

    for device in [core_dev, x_dev, y_dev] + partners[4:]:
        greet(device)

    @pl.when(plane < planes - 1)
    def _():
        greet(up_dev)

    @pl.when(plane > 0)
    def _():
        greet(down_dev)

    keep = pltpu.make_async_copy(leaves_ref, own.at[plane * 2 + core], local_sem)
    keep.start()
    keep.wait()
    pl.semaphore_wait(
        barrier,
        3 + len(partners[4:]) + jnp.where(plane < planes - 1, 1, 0) + jnp.where(plane > 0, 1, 0),
    )

    def copy(source, target, at, side, part, send_sem, device):
        piece = pl.ds(part * half, half)
        return pltpu.make_async_remote_copy(
            src_ref=held[source].at[at * 2 + side, piece],
            dst_ref=held[target].at[at * 2 + side, piece],
            send_sem=send_sem,
            recv_sem=recv.at[target, at * 2 + side, part],
            device_id=(device,),
            device_id_type=pl.DeviceIdType.MESH,
        )

    def to_core(column, at, part):
        return copy(column, column, at, core, part, send_core.at[column, at, part], core_dev)

    def to_x(column, at, part):
        row = part if column == 0 else 2
        return copy(column, column + 1, at, core, part, send_x.at[row, at], x_dev)

    def to_y(column, at, part):
        row = part if column == 0 else 2
        return copy(column, column + 2, at, core, part, send_y.at[row, at], y_dev)

    def to_up(at, part):
        return copy(0, 0, at, core, part, send_up.at[at, part], up_dev)

    def to_down(at, part):
        return copy(0, 0, at, core, part, send_down.at[at, part], down_dev)

    def arrived(column, at, side, part):
        copy(column, column, at, side, part, send_core.at[column, at, part], core_dev).wait_recv()

    def spread(at, part):
        to_x(0, at, part).start()
        to_y(0, at, part).start()
        to_core(0, at, part).start()

    def line_step(step):
        for part in range(2):
            @pl.when(plane - step >= 0)
            def _():
                arrived(0, plane - step, core, part)

                @pl.when(plane < planes - 1)
                def _():
                    to_up(plane - step, part).start()
                spread(plane - step, part)

            @pl.when(plane + step < planes)
            def _():
                arrived(0, plane + step, core, part)

                @pl.when(plane > 0)
                def _():
                    to_down(plane + step, part).start()
                spread(plane + step, part)

    def at_distance(step, action):
        if step == 0:
            action(plane)
            return

        @pl.when(plane - step >= 0)
        def _():
            action(plane - step)

        @pl.when(plane + step < planes)
        def _():
            action(plane + step)

    def side_step(step):
        def action(at):
            for part in range(2):
                for column in (1, 2):
                    arrived(column, at, core, part)
                    if column == 1 and part == 0:
                        to_y(column, at, part).start()
                    if column == 2 and part == 1:
                        to_x(column, at, part).start()
                    to_core(column, at, part).start()
        at_distance(step, action)

    def across_step(step):
        def action(at):
            for part in range(2):
                arrived(3, at, core, part)
                to_core(3, at, part).start()
        at_distance(step, action)

    def node_copy(level):
        return pltpu.make_async_remote_copy(
            src_ref=mine.at[level],
            dst_ref=sibling.at[level],
            send_sem=node_send.at[level],
            recv_sem=node_recv.at[level],
            device_id=(partners[level],),
            device_id_type=pl.DeviceIdType.MESH,
        )

    def columns(leaf):
        return pl.ds(pl.multiple_of(leaf * LEAF, LEAF), LEAF)

    def self_leaf(leaf, carry):
        target = target_side(leaves_ref[leaf, :D, :])
        targets[leaf] = target
        near_ref[:, columns(leaf)] = tile_term(
            target, leaves_ref[leaf, :D, :], leaves_ref[leaf, D:, :]
        ).T
        far_ref[:, columns(leaf)] = jnp.zeros((RHS, LEAF), jnp.float32)
        return carry

    def far_levels(first, last):
        def item(index, carry):
            level = first + index // leaves_dev
            leaf = index % leaves_dev
            term = tile_term(targets[leaf], sibling[level, :D, :], sibling[level, D:, :])
            far_ref[:, columns(leaf)] += term.T
            return carry
        lax.fori_loop(0, (last - first) * leaves_dev, item, 0)

    def next_node(level):
        node_copy(level).wait_recv()
        if level + 1 < depth_count:
            mine[level + 1] = merged(mine[level], sibling[level], bits[level])
            node_copy(level + 1).start()

    def near_column(column):
        for at in range(planes):
            for part in range(2):
                arrived(column, at, 1 - core, part)

        def item(index, carry):
            spot = column * cap + index
            target, place, leaf = item_ref[0, spot], item_ref[1, spot], item_ref[2, spot]
            block = held[column][place, leaf]
            results[spot] = tile_term(targets[target], block[:D], block[D:]).T
            return carry
        lax.fori_loop(0, caps[column], item, 0)

    mine[0] = base_ref[...]
    node_copy(0).start()
    for part in range(2):
        @pl.when(plane < planes - 1)
        def _():
            to_up(plane, part).start()

        @pl.when(plane > 0)
        def _():
            to_down(plane, part).start()
        spread(plane, part)
    results[4 * cap] = jnp.zeros((RHS, LEAF), jnp.float32)
    lax.fori_loop(0, leaves_dev, self_leaf, 0)
    early = min(3, depth_count)
    for level in range(early):
        next_node(level)
    far_levels(0, early)
    line_step(1)
    side_step(0)
    for level in range(early, depth_count):
        next_node(level)
    far_levels(early, depth_count)
    for step in range(2, planes):
        line_step(step)
        side_step(step - 1)
    near_column(0)
    side_step(planes - 1)
    near_column(1)
    near_column(2)
    for step in range(planes):
        across_step(step)
    near_column(3)

    def finish(leaf, carry):
        total = near_ref[:, columns(leaf)]
        for slot in range(NEAR):
            total = total + results[spot_ref[leaf * NEAR + slot]]
        near_ref[:, columns(leaf)] = total * near_scale
        far_ref[:, columns(leaf)] = far_ref[:, columns(leaf)] * far_scale
        return carry
    lax.fori_loop(0, leaves_dev, finish, 0)

    for level in range(depth_count):
        node_copy(level).wait_send()
    for at in range(planes):
        for part in range(2):
            to_x(0, at, part).wait_send()
            to_y(0, at, part).wait_send()
            for column in range(4):
                to_core(column, at, part).wait_send()

            @pl.when((plane < planes - 1) & (plane >= at))
            def _():
                to_up(at, part).wait_send()

            @pl.when((plane > 0) & (plane <= at))
            def _():
                to_down(at, part).wait_send()
        to_y(1, at, 0).wait_send()
        to_x(2, at, 1).wait_send()


def fused(leaf_blocks, base_node, near_leaf, near_count, n_dev, my_index):
    leaves_dev = leaf_blocks.shape[0]
    p_dev = leaves_dev * LEAF
    slot_count = leaves_dev * NEAR
    depth_count = n_dev.bit_length() - 1
    planes = n_dev // 8
    column_devs = 2 * planes
    runs = [min(n_dev - 1, slot_count - at) for at in range(0, slot_count, n_dev - 1)]
    caps = [sum(min(run, column_devs - (column == 0)) for run in runs) for column in range(4)]
    cap = max(caps)

    my_leaf = lax.dynamic_slice_in_dim(near_leaf, my_index * leaves_dev, leaves_dev).reshape(-1)
    my_count = lax.dynamic_slice_in_dim(near_count, my_index * leaves_dev, leaves_dev)
    slot = jnp.arange(slot_count, dtype=jnp.int32)
    live = slot % NEAR < jnp.repeat(my_count, NEAR)
    owner = my_leaf // leaves_dev
    column = (owner // 2 % 4) ^ (my_index // 2 % 4)
    earlier = (slot[None, :] < slot[:, None]) & live[None, :] & (column[None, :] == column[:, None])
    rank = jnp.sum(earlier.astype(jnp.int32), axis=1)
    spot = jnp.where(live, column * cap + rank, 4 * cap).astype(jnp.int32)
    fields = jnp.stack([slot // NEAR, owner // 8 * 2 + owner % 2, my_leaf % leaves_dev])
    chosen = spot[None, :] == jnp.arange(4 * cap, dtype=jnp.int32)[:, None]
    items = jnp.sum(jnp.where(chosen[None], fields[:, None, :], 0), axis=2).astype(jnp.int32)

    tiles = leaves_dev * (depth_count + 1) + sum(caps)
    whole = pl.BlockSpec(memory_space=pltpu.VMEM)
    scalars = pl.BlockSpec(memory_space=pltpu.SMEM)
    dma = pltpu.SemaphoreType.DMA
    column_buffer = pltpu.VMEM((column_devs, leaves_dev, ROWS, LEAF), jnp.bfloat16)
    return pl.pallas_call(
        functools.partial(
            fused_kernel, n_dev, tuple(caps), 4.0 / math.sqrt(LEAF * (NEAR + 1)),
            4.0 / math.sqrt(p_dev * n_dev),
        ),
        in_specs=[scalars, scalars, whole, whole],
        out_specs=[whole, whole],
        out_shape=[jax.ShapeDtypeStruct((RHS, p_dev), jnp.float32)] * 2,
        scratch_shapes=[
            column_buffer, column_buffer, column_buffer, column_buffer,
            pltpu.VMEM((leaves_dev, LEAF, DEPTH), jnp.bfloat16),
            pltpu.VMEM((4 * cap + 1, RHS, LEAF), jnp.float32),
            pltpu.VMEM((depth_count, ROWS, SKEL), jnp.bfloat16),
            pltpu.VMEM((depth_count, ROWS, SKEL), jnp.bfloat16),
            dma((4, column_devs, 2)),
            dma((3, planes)),
            dma((3, planes)),
            dma((4, planes, 2)),
            dma((planes, 2)),
            dma((planes, 2)),
            dma((depth_count,)),
            dma((depth_count,)),
            dma,
        ],
        compiler_params=pltpu.CompilerParams(
            collective_id=0, has_side_effects=True, vmem_limit_bytes=56 * 2**20
        ),
        cost_estimate=pl.CostEstimate(
            flops=tiles * 2 * LEAF * LEAF * (DEPTH + 256),
            bytes_accessed=4 * 2**20,
            transcendentals=tiles * LEAF * LEAF,
        ),
        name="exchange_and_tiles",
    )(items, spot, leaf_blocks, base_node)


def fold_child(nodes):
    half = nodes.shape[-1] // 2
    folded = nodes[..., D:, :half].astype(jnp.float32) + nodes[..., D:, half:].astype(jnp.float32)
    return jnp.concatenate([nodes[..., :D, :half], folded.astype(jnp.bfloat16)], axis=-2)


def sibling_nodes(nodes, my_index, depth_count):
    found = []
    for level in range(depth_count):
        found.append(lax.dynamic_index_in_dim(nodes, (my_index >> level) ^ 1, 0, keepdims=False))
        if level + 1 < depth_count:
            child = fold_child(nodes)
            nodes = jnp.concatenate([child[0::2], child[1::2]], axis=-1)
    return jnp.stack(found)


def per_device(points, weights, skel_index, assign, near_leaf, near_count):
    n_dev = lax.axis_size("leaf")
    my_index = lax.axis_index("leaf")
    depth_count = n_dev.bit_length() - 1
    p_dev = points.shape[1]
    leaves_dev = p_dev // LEAF

    member = (assign[None, :] == jnp.arange(SKEL, dtype=jnp.int32)[:, None]).astype(jnp.bfloat16)
    base_weights = lax.dot_general(
        weights, member, (((1,), (1,)), ((), ())), preferred_element_type=jnp.float32
    )
    base_node = jnp.concatenate([points[:, skel_index], base_weights.astype(jnp.bfloat16)], axis=0)
    stacked = jnp.concatenate([points, weights], axis=0)
    if n_dev >= 16 and n_dev * stacked.size * 2 <= FITS:
        leaf_blocks = stacked.reshape(ROWS, leaves_dev, LEAF).transpose(1, 0, 2)
        return fused(leaf_blocks, base_node, near_leaf, near_count, n_dev, my_index)
    base_node, stacked = lax.optimization_barrier((base_node, stacked))
    nodes = lax.all_gather(base_node, "leaf")
    blocks = lax.all_gather(stacked, "leaf")

    slot_count = leaves_dev * NEAR
    my_leaf = lax.dynamic_slice_in_dim(near_leaf, my_index * leaves_dev, leaves_dev).reshape(-1)
    my_count = lax.dynamic_slice_in_dim(near_count, my_index * leaves_dev, leaves_dev)
    before = jnp.arange(leaves_dev + 1)[:, None] > jnp.arange(leaves_dev)[None, :]
    start = jnp.sum(jnp.where(before, my_count[None, :], 0), axis=1).astype(jnp.int32)
    slot = jnp.arange(slot_count, dtype=jnp.int32)
    live = slot % NEAR < jnp.repeat(my_count, NEAR)
    spot = jnp.where(live, jnp.repeat(start[:-1], NEAR) + slot % NEAR, slot_count)
    chosen = spot[None, :] == slot[:, None]
    item_leaf = jnp.sum(jnp.where(chosen, my_leaf[None, :], 0), axis=1).astype(jnp.int32)

    siblings = sibling_nodes(nodes, my_index, depth_count)
    tile_flops = 2 * LEAF * LEAF * (DEPTH + 256)
    column_block = lambda rows: pl.BlockSpec((rows, LEAF), lambda leaf: (0, leaf))
    self_term, far_field = pl.pallas_call(
        functools.partial(local_kernel, depth_count, 4.0 / math.sqrt(p_dev * n_dev)),
        grid=(leaves_dev,),
        in_specs=[
            column_block(D),
            column_block(RHS),
            pl.BlockSpec((depth_count, ROWS, SKEL), lambda leaf: (0, 0, 0)),
        ],
        out_specs=[column_block(RHS), column_block(RHS)],
        out_shape=[jax.ShapeDtypeStruct((RHS, p_dev), jnp.float32)] * 2,
        compiler_params=pltpu.CompilerParams(vmem_limit_bytes=48 * 2**20),
        cost_estimate=pl.CostEstimate(
            flops=leaves_dev * (depth_count + 1) * tile_flops,
            bytes_accessed=4 * 2**20,
            transcendentals=leaves_dev * (depth_count + 1) * LEAF * LEAF,
        ),
        name="local_and_far",
    )(points, weights, siblings)

    whole = pl.BlockSpec(memory_space=pltpu.VMEM)
    scalars = pl.BlockSpec(memory_space=pltpu.SMEM)
    near_field = pl.pallas_call(
        functools.partial(near_kernel, leaves_dev, 4.0 / math.sqrt(LEAF * (NEAR + 1))),
        in_specs=[scalars, scalars, scalars, whole, whole, pl.BlockSpec(memory_space=pl.ANY)],
        out_specs=whole,
        out_shape=jax.ShapeDtypeStruct((RHS, p_dev), jnp.float32),
        scratch_shapes=[
            pltpu.VMEM((SLOTS, ROWS, LEAF), jnp.bfloat16),
            pltpu.SemaphoreType.DMA((SLOTS,)),
        ],
        compiler_params=pltpu.CompilerParams(vmem_limit_bytes=48 * 2**20),
        cost_estimate=pl.CostEstimate(
            flops=slot_count * tile_flops,
            bytes_accessed=slot_count * ROWS * LEAF * 2,
            transcendentals=slot_count * LEAF * LEAF,
        ),
        name="near_blocks",
    )(item_leaf // leaves_dev, item_leaf % leaves_dev, start, points, self_term, blocks)
    return (near_field, far_field)


def solution(mesh):
    return jax.shard_map(
        per_device,
        mesh=mesh,
        in_specs=(P(None, "leaf"), P(None, "leaf"), P("leaf"), P("leaf"), P(), P()),
        out_specs=(P(None, "leaf"), P(None, "leaf")),
        check_vma=False,
    )
```

```python
import functools
import math

import jax
import jax.numpy as jnp
from jax import lax
from jax.experimental import pallas as pl
from jax.experimental.pallas import tpu as pltpu
from jax.sharding import PartitionSpec as P

D = 64
RHS = 32
LEAF = 512
SKEL = 512
NEAR = 12
ROWS = D + RHS
DEPTH = 256
SCALE2 = 1.0 / (D * math.log(2.0))
SLOTS = 4
PER_PAIR = 4


def three_parts(x):
    high = x.astype(jnp.bfloat16).astype(jnp.float32)
    rest = x - high
    mid = rest.astype(jnp.bfloat16).astype(jnp.float32)
    low = (rest - mid).astype(jnp.bfloat16).astype(jnp.float32)
    return high, mid, low


def neg_norm_parts(points32):
    norm = jnp.sum(points32 * points32, axis=0, keepdims=True) * (-SCALE2)
    return three_parts(norm)


def tail_rows(parts, first, ones_first, rows):
    row = lax.broadcasted_iota(jnp.int32, (rows, parts[0].shape[1]), 0)
    tail = jnp.where((row >= ones_first) & (row < ones_first + 3), 1.0, 0.0)
    for step, part in enumerate(parts):
        tail = jnp.where(row == first + step, part, tail)
    return tail


def target_side(points):
    points32 = points.astype(jnp.float32)
    parts = three_parts(points32 * (2.0 * SCALE2))
    tail = tail_rows(neg_norm_parts(points32), 3, 0, DEPTH - 3 * D)
    return jnp.concatenate([*parts, tail], axis=0).T.astype(jnp.bfloat16)


def source_side(points):
    tail = tail_rows(neg_norm_parts(points.astype(jnp.float32)), 0, 3, DEPTH - 3 * D)
    return jnp.concatenate([points, points, points, tail.astype(jnp.bfloat16)], axis=0)


def tile_term(target, points, weights):
    exponent = jnp.dot(target, source_side(points), preferred_element_type=jnp.float32)
    tile = jnp.exp2(exponent).astype(jnp.bfloat16)
    return lax.dot_general(
        tile, weights, (((1,), (1,)), ((), ())), preferred_element_type=jnp.float32
    )


def local_kernel(depth_count, far_scale, points_ref, weights_ref, nodes_ref, self_ref, far_ref):
    points = points_ref[...]
    target = target_side(points)
    self_ref[...] = tile_term(target, points, weights_ref[...]).T
    total = jnp.zeros((LEAF, RHS), jnp.float32)
    for level in range(depth_count):
        total = total + tile_term(target, nodes_ref[level, :D, :], nodes_ref[level, D:, :])
    far_ref[...] = total.T * far_scale


def near_kernel(leaves_dev, near_scale, owner_ref, place_ref, start_ref, points_ref, self_ref,
                blocks_ref, out_ref, held, sems):
    total_items = start_ref[leaves_dev]

    def fetch(item):
        slot = lax.rem(item, SLOTS)
        column = pl.multiple_of(place_ref[item] * LEAF, LEAF)
        return pltpu.make_async_copy(
            blocks_ref.at[owner_ref[item], :, pl.ds(column, LEAF)], held.at[slot], sems.at[slot]
        )

    for ahead in range(SLOTS - 1):
        @pl.when(ahead < total_items)
        def _():
            fetch(ahead).start()

    def leaf_step(leaf, carry):
        columns = pl.ds(pl.multiple_of(leaf * LEAF, LEAF), LEAF)
        target = target_side(points_ref[:, columns])

        def item_step(item, running):
            @pl.when(item + SLOTS - 1 < total_items)
            def _():
                fetch(item + SLOTS - 1).start()
            fetch(item).wait()
            slot = lax.rem(item, SLOTS)
            return running + tile_term(target, held[slot, :D, :], held[slot, D:, :])

        total = lax.fori_loop(
            start_ref[leaf], start_ref[leaf + 1], item_step, jnp.zeros((LEAF, RHS), jnp.float32)
        )
        out_ref[:, columns] = (total.T + self_ref[:, columns]) * near_scale
        return carry

    lax.fori_loop(0, leaves_dev, leaf_step, 0)


def merged(mine, sibling, upper_bit):
    half = SKEL // 2
    parts = []
    for node in (mine, sibling):
        weights = node[D:, :half].astype(jnp.float32) + node[D:, half:].astype(jnp.float32)
        parts.append(
            jnp.concatenate([node[:D, :half].astype(jnp.float32), weights], axis=0)
        )
    lower = jnp.where(upper_bit == 0, parts[0], parts[1])
    upper = jnp.where(upper_bit == 0, parts[1], parts[0])
    return jnp.concatenate([lower, upper], axis=1).astype(jnp.bfloat16)


def layer_kernel(n_dev, near_scale, far_scale, item_ref, spot_ref, leaves_ref, base_ref,
                 near_ref, far_ref, below1, above1, below2, above2, below3, above3, points,
                 targets, results, outbox, inbox, mine, sibling, line_recv, line_send,
                 point_send, point_recv, sum_send, sum_recv, node_send, node_recv):
    planes = n_dev // 8
    depth_count = n_dev.bit_length() - 1
    leaves_dev = leaves_ref.shape[0]
    half = leaves_dev // 2
    held = (leaves_ref, below1, above1, below2, above2, below3, above3)
    me = lax.axis_index("leaf")
    bits = [(me // 2**level) % 2 for level in range(depth_count)]
    partners = [me + (1 - 2 * bits[level]) * 2**level for level in range(depth_count)]
    plane = me // 8

    def peer(apart):
        found = me
        for level in range(3):
            found = found + (1 - 2 * bits[level]) * 2**level * (apart // 2**level % 2)
        return found

    def remote(source, target, send_sem, recv_sem, device):
        return pltpu.make_async_remote_copy(
            src_ref=source, dst_ref=target, send_sem=send_sem, recv_sem=recv_sem,
            device_id=(device,), device_id_type=pl.DeviceIdType.MESH,
        )

    barrier = pltpu.get_barrier_semaphore()

    def greet(device):
        pl.semaphore_signal(
            barrier, inc=1, device_id=(device,), device_id_type=pl.DeviceIdType.MESH
        )

    for device in [peer(apart) for apart in range(1, 8)] + partners[4:]:
        greet(device)

    @pl.when(plane < planes - 1)
    def _():
        greet(me + 8)

    @pl.when(plane > 0)
    def _():
        greet(me - 8)

    pl.semaphore_wait(
        barrier,
        7 + len(partners[4:]) + jnp.where(plane < planes - 1, 1, 0) + jnp.where(plane > 0, 1, 0),
    )

    def line_copy(step, above, part):
        target = 2 * step - 1 + above
        source = 0 if step == 1 else target - 2
        piece = pl.ds(part * half, half)
        return remote(
            held[source].at[piece], held[target].at[piece], line_send.at[target - 1, part],
            line_recv.at[target - 1, part], me - 8 if above else me + 8,
        )

    def sends(step, above):
        if above:
            return (plane > 0) & (plane + step - 1 < planes)
        return (plane < planes - 1) & (plane - step + 1 >= 0)

    def receives(step, above):
        return plane + step < planes if above else plane - step >= 0

    def line_step(step):
        for part in range(2):
            for above in range(2):
                @pl.when(receives(step, above))
                def _():
                    line_copy(step, above, part).wait_recv()
                if step + 1 < planes:
                    @pl.when(sends(step + 1, above))
                    def _():
                        line_copy(step + 1, above, part).start()

    def point_copy(apart):
        return remote(
            leaves_ref.at[:, pl.ds(0, D)], points.at[apart], point_send.at[apart],
            point_recv.at[apart], peer(apart),
        )

    def sum_copy(apart):
        return remote(
            outbox.at[apart], inbox.at[apart], sum_send.at[apart], sum_recv.at[apart], peer(apart)
        )

    def node_copy(level):
        return remote(
            mine.at[level], sibling.at[level], node_send.at[level], node_recv.at[level],
            partners[level],
        )

    def columns(leaf):
        return pl.ds(pl.multiple_of(leaf * LEAF, LEAF), LEAF)

    def self_leaf(leaf, carry):
        target = target_side(leaves_ref[leaf, :D, :])
        targets[leaf] = target
        near_ref[:, columns(leaf)] = tile_term(
            target, leaves_ref[leaf, :D, :], leaves_ref[leaf, D:, :]
        ).T
        far_ref[:, columns(leaf)] = jnp.zeros((RHS, LEAF), jnp.float32)
        return carry

    def far_levels(first, last):
        def item(index, carry):
            level = first + index // leaves_dev
            leaf = index % leaves_dev
            term = tile_term(targets[leaf], sibling[level, :D, :], sibling[level, D:, :])
            far_ref[:, columns(leaf)] += term.T
            return carry
        lax.fori_loop(0, (last - first) * leaves_dev, item, 0)

    def next_node(level):
        node_copy(level).wait_recv()
        if level + 1 < depth_count:
            mine[level + 1] = merged(mine[level], sibling[level], bits[level])
            node_copy(level + 1).start()

    def prepare(apart, carry):
        point_copy(apart).wait_recv()

        def one_leaf(leaf, inner):
            targets[apart * leaves_dev + leaf] = target_side(points[apart, leaf])
            return inner
        return lax.fori_loop(0, leaves_dev, one_leaf, carry)

    def finish(apart):
        def leaf_sum(leaf):
            first = (apart * leaves_dev + leaf) * NEAR
            total = results[spot_ref[first]]
            for slot in range(1, NEAR):
                total = total + results[spot_ref[first + slot]]
            return total

        @pl.when(apart == 0)
        def _():
            def own_leaf(leaf, carry):
                near_ref[:, columns(leaf)] += leaf_sum(leaf)
                return carry
            lax.fori_loop(0, leaves_dev, own_leaf, 0)

        @pl.when(apart > 0)
        def _():
            def peer_leaf(leaf, carry):
                outbox[apart, :, columns(leaf)] = leaf_sum(leaf).astype(jnp.bfloat16)
                return carry
            lax.fori_loop(0, leaves_dev, peer_leaf, 0)
            sum_copy(apart).start()

    def near_group(group, is_last):
        def readers(index, carry):
            apart = 7 - index

            def item(rank, inner):
                spot = (group * 8 + apart) * PER_PAIR + rank
                block = held[group][item_ref[1, spot]]
                target = targets[apart * leaves_dev + item_ref[0, spot]]
                results[spot] = tile_term(target, block[:D], block[D:]).T
                return inner
            lax.fori_loop(0, PER_PAIR, item, 0)
            if is_last is not None:
                @pl.when(is_last)
                def _():
                    finish(apart)
            return carry
        lax.fori_loop(0, 7 if group == 0 else 8, readers, 0)

    def line_groups(step):
        for above in range(2):
            @pl.when(receives(step, above))
            def _():
                last = None
                if step >= planes // 2:
                    farther = plane < planes - 1 - plane
                    reach = jnp.where(farther, planes - 1 - plane, plane)
                    side = jnp.where(farther, 1, 0)
                    last = (reach == step) & (side == above)
                near_group(2 * step - 1 + above, last)

    for part in range(2):
        for above in range(2):
            @pl.when(sends(1, above))
            def _():
                line_copy(1, above, part).start()
    mine[0] = base_ref[...]
    node_copy(0).start()
    for apart in range(1, 8):
        point_copy(apart).start()
    results[7 * 8 * PER_PAIR] = jnp.zeros((RHS, LEAF), jnp.float32)
    lax.fori_loop(0, leaves_dev, self_leaf, 0)
    early = min(3, depth_count)
    for level in range(early):
        next_node(level)
    far_levels(0, early)
    line_step(1)
    for level in range(early, depth_count):
        next_node(level)
    far_levels(early, depth_count)
    lax.fori_loop(1, 8, prepare, 0)
    near_group(0, None)
    for step in range(2, planes):
        line_step(step)
        line_groups(step - 1)
    line_groups(planes - 1)

    for apart in range(1, 8):
        sum_copy(apart).wait_recv()

    def scale(leaf, carry):
        total = near_ref[:, columns(leaf)]
        for apart in range(1, 8):
            total = total + inbox[apart, :, columns(leaf)].astype(jnp.float32)
        near_ref[:, columns(leaf)] = total * near_scale
        far_ref[:, columns(leaf)] = far_ref[:, columns(leaf)] * far_scale
        return carry
    lax.fori_loop(0, leaves_dev, scale, 0)

    for level in range(depth_count):
        node_copy(level).wait_send()
    for apart in range(1, 8):
        point_copy(apart).wait_send()
        sum_copy(apart).wait_send()
    for step in range(1, planes):
        for part in range(2):
            for above in range(2):
                @pl.when(sends(step, above))
                def _():
                    line_copy(step, above, part).wait_send()


def fused(leaf_blocks, base_node, near_leaf, near_count, n_dev, my_index):
    leaves_dev = leaf_blocks.shape[0]
    p_dev = leaves_dev * LEAF
    slot_count = leaves_dev * NEAR
    depth_count = n_dev.bit_length() - 1
    planes = n_dev // 8
    spots = 7 * 8 * PER_PAIR

    readers = my_index ^ jnp.arange(8, dtype=jnp.int32)
    leaf_ids = near_leaf.reshape(n_dev, slot_count)[readers]
    counts = near_count.reshape(n_dev, leaves_dev)[readers]
    slot = jnp.arange(slot_count, dtype=jnp.int32)
    owner = leaf_ids // leaves_dev
    live = slot % NEAR < jnp.repeat(counts, NEAR, axis=1)
    live = live & (owner % 8 == my_index % 8)
    apart = owner // 8 - my_index // 8
    group = jnp.where(apart == 0, 0, 2 * jnp.abs(apart) - jnp.where(apart < 0, 1, 0))
    earlier = (slot[None, :] < slot[:, None])[None] & live[:, None, :]
    earlier = earlier & (group[:, None, :] == group[:, :, None])
    rank = jnp.sum(earlier.astype(jnp.int32), axis=2)
    reader = jnp.arange(8, dtype=jnp.int32)[:, None]
    spot = jnp.where(live, (group * 8 + reader) * PER_PAIR + rank, spots).astype(jnp.int32)
    fields = (slot[None, :] // NEAR) * leaves_dev + leaf_ids % leaves_dev
    spot = spot.reshape(-1)
    chosen = spot[None, :] == jnp.arange(spots, dtype=jnp.int32)[:, None]
    packed = jnp.sum(jnp.where(chosen, fields.reshape(1, -1), 0), axis=1).astype(jnp.int32)
    items = jnp.stack([packed // leaves_dev, packed % leaves_dev])

    tiles = leaves_dev * (depth_count + 1) + planes * 8 * PER_PAIR
    whole = pl.BlockSpec(memory_space=pltpu.VMEM)
    scalars = pl.BlockSpec(memory_space=pltpu.SMEM)
    dma = pltpu.SemaphoreType.DMA
    block_buffer = pltpu.VMEM((leaves_dev, ROWS, LEAF), jnp.bfloat16)
    return pl.pallas_call(
        functools.partial(
            layer_kernel, n_dev, 4.0 / math.sqrt(LEAF * (NEAR + 1)),
            4.0 / math.sqrt(p_dev * n_dev),
        ),
        in_specs=[scalars, scalars, whole, whole],
        out_specs=[whole, whole],
        out_shape=[jax.ShapeDtypeStruct((RHS, p_dev), jnp.float32)] * 2,
        scratch_shapes=[
            *[block_buffer] * 6,
            pltpu.VMEM((8, leaves_dev, D, LEAF), jnp.bfloat16),
            pltpu.VMEM((8 * leaves_dev, LEAF, DEPTH), jnp.bfloat16),
            pltpu.VMEM((spots + 1, RHS, LEAF), jnp.float32),
            pltpu.VMEM((8, RHS, p_dev), jnp.bfloat16),
            pltpu.VMEM((8, RHS, p_dev), jnp.bfloat16),
            pltpu.VMEM((depth_count, ROWS, SKEL), jnp.bfloat16),
            pltpu.VMEM((depth_count, ROWS, SKEL), jnp.bfloat16),
            dma((6, 2)),
            dma((6, 2)),
            dma((8,)),
            dma((8,)),
            dma((8,)),
            dma((8,)),
            dma((depth_count,)),
            dma((depth_count,)),
        ],
        compiler_params=pltpu.CompilerParams(
            collective_id=0, has_side_effects=True, vmem_limit_bytes=60 * 2**20
        ),
        cost_estimate=pl.CostEstimate(
            flops=tiles * 2 * LEAF * LEAF * (DEPTH + 256),
            bytes_accessed=4 * 2**20,
            transcendentals=tiles * LEAF * LEAF,
        ),
        name="exchange_and_tiles",
    )(items, spot, leaf_blocks, base_node)


def fold_child(nodes):
    half = nodes.shape[-1] // 2
    folded = nodes[..., D:, :half].astype(jnp.float32) + nodes[..., D:, half:].astype(jnp.float32)
    return jnp.concatenate([nodes[..., :D, :half], folded.astype(jnp.bfloat16)], axis=-2)


def sibling_nodes(nodes, my_index, depth_count):
    found = []
    for level in range(depth_count):
        found.append(lax.dynamic_index_in_dim(nodes, (my_index >> level) ^ 1, 0, keepdims=False))
        if level + 1 < depth_count:
            child = fold_child(nodes)
            nodes = jnp.concatenate([child[0::2], child[1::2]], axis=-1)
    return jnp.stack(found)


def per_device(points, weights, skel_index, assign, near_leaf, near_count):
    n_dev = lax.axis_size("leaf")
    my_index = lax.axis_index("leaf")
    depth_count = n_dev.bit_length() - 1
    p_dev = points.shape[1]
    leaves_dev = p_dev // LEAF

    member = (assign[None, :] == jnp.arange(SKEL, dtype=jnp.int32)[:, None]).astype(jnp.bfloat16)
    base_weights = lax.dot_general(
        weights, member, (((1,), (1,)), ((), ())), preferred_element_type=jnp.float32
    )
    base_node = jnp.concatenate([points[:, skel_index], base_weights.astype(jnp.bfloat16)], axis=0)
    stacked = jnp.concatenate([points, weights], axis=0)
    if n_dev == 32 and PER_PAIR * (n_dev - 1) >= leaves_dev * NEAR:
        leaf_blocks = stacked.reshape(ROWS, leaves_dev, LEAF).transpose(1, 0, 2)
        return fused(leaf_blocks, base_node, near_leaf, near_count, n_dev, my_index)
    base_node, stacked = lax.optimization_barrier((base_node, stacked))
    nodes = lax.all_gather(base_node, "leaf")
    blocks = lax.all_gather(stacked, "leaf")

    slot_count = leaves_dev * NEAR
    my_leaf = lax.dynamic_slice_in_dim(near_leaf, my_index * leaves_dev, leaves_dev).reshape(-1)
    my_count = lax.dynamic_slice_in_dim(near_count, my_index * leaves_dev, leaves_dev)
    before = jnp.arange(leaves_dev + 1)[:, None] > jnp.arange(leaves_dev)[None, :]
    start = jnp.sum(jnp.where(before, my_count[None, :], 0), axis=1).astype(jnp.int32)
    slot = jnp.arange(slot_count, dtype=jnp.int32)
    live = slot % NEAR < jnp.repeat(my_count, NEAR)
    spot = jnp.where(live, jnp.repeat(start[:-1], NEAR) + slot % NEAR, slot_count)
    chosen = spot[None, :] == slot[:, None]
    item_leaf = jnp.sum(jnp.where(chosen, my_leaf[None, :], 0), axis=1).astype(jnp.int32)

    siblings = sibling_nodes(nodes, my_index, depth_count)
    tile_flops = 2 * LEAF * LEAF * (DEPTH + 256)
    column_block = lambda rows: pl.BlockSpec((rows, LEAF), lambda leaf: (0, leaf))
    self_term, far_field = pl.pallas_call(
        functools.partial(local_kernel, depth_count, 4.0 / math.sqrt(p_dev * n_dev)),
        grid=(leaves_dev,),
        in_specs=[
            column_block(D),
            column_block(RHS),
            pl.BlockSpec((depth_count, ROWS, SKEL), lambda leaf: (0, 0, 0)),
        ],
        out_specs=[column_block(RHS), column_block(RHS)],
        out_shape=[jax.ShapeDtypeStruct((RHS, p_dev), jnp.float32)] * 2,
        compiler_params=pltpu.CompilerParams(vmem_limit_bytes=48 * 2**20),
        cost_estimate=pl.CostEstimate(
            flops=leaves_dev * (depth_count + 1) * tile_flops,
            bytes_accessed=4 * 2**20,
            transcendentals=leaves_dev * (depth_count + 1) * LEAF * LEAF,
        ),
        name="local_and_far",
    )(points, weights, siblings)

    whole = pl.BlockSpec(memory_space=pltpu.VMEM)
    scalars = pl.BlockSpec(memory_space=pltpu.SMEM)
    near_field = pl.pallas_call(
        functools.partial(near_kernel, leaves_dev, 4.0 / math.sqrt(LEAF * (NEAR + 1))),
        in_specs=[scalars, scalars, scalars, whole, whole, pl.BlockSpec(memory_space=pl.ANY)],
        out_specs=whole,
        out_shape=jax.ShapeDtypeStruct((RHS, p_dev), jnp.float32),
        scratch_shapes=[
            pltpu.VMEM((SLOTS, ROWS, LEAF), jnp.bfloat16),
            pltpu.SemaphoreType.DMA((SLOTS,)),
        ],
        compiler_params=pltpu.CompilerParams(vmem_limit_bytes=48 * 2**20),
        cost_estimate=pl.CostEstimate(
            flops=slot_count * tile_flops,
            bytes_accessed=slot_count * ROWS * LEAF * 2,
            transcendentals=slot_count * LEAF * LEAF,
        ),
        name="near_blocks",
    )(item_leaf // leaves_dev, item_leaf % leaves_dev, start, points, self_term, blocks)
    return (near_field, far_field)


def solution(mesh):
    return jax.shard_map(
        per_device,
        mesh=mesh,
        in_specs=(P(None, "leaf"), P(None, "leaf"), P("leaf"), P("leaf"), P(), P()),
        out_specs=(P(None, "leaf"), P(None, "leaf")),
        check_vma=False,
    )
```

```python
import functools
import math

import jax
import jax.numpy as jnp
from jax import lax
from jax.experimental import pallas as pl
from jax.experimental.pallas import tpu as pltpu
from jax.sharding import PartitionSpec as P

D = 64
RHS = 32
LEAF = 512
SKEL = 512
NEAR = 12
ROWS = D + RHS
DEPTH = 256
SCALE2 = 1.0 / (D * math.log(2.0))
SLOTS = 4
TAIL = 16
PER_PAIR = 4


def three_parts(x):
    high = x.astype(jnp.bfloat16).astype(jnp.float32)
    rest = x - high
    mid = rest.astype(jnp.bfloat16).astype(jnp.float32)
    low = (rest - mid).astype(jnp.bfloat16).astype(jnp.float32)
    return high, mid, low


def neg_norm_parts(points32):
    norm = jnp.sum(points32 * points32, axis=0, keepdims=True) * (-SCALE2)
    return three_parts(norm)


def tail_rows(parts, first, ones_first, rows):
    row = lax.broadcasted_iota(jnp.int32, (rows, parts[0].shape[1]), 0)
    tail = jnp.where((row >= ones_first) & (row < ones_first + 3), 1.0, 0.0)
    for step, part in enumerate(parts):
        tail = jnp.where(row == first + step, part, tail)
    return tail


def spare_rows(points):
    return jnp.zeros((DEPTH - 3 * D - TAIL, points.shape[1]), jnp.bfloat16)


def target_side(points):
    points32 = points.astype(jnp.float32)
    parts = three_parts(points32 * (2.0 * SCALE2))
    tail = tail_rows(neg_norm_parts(points32), 3, 0, TAIL)
    rows = [part.astype(jnp.bfloat16) for part in (*parts, tail)]
    return jnp.concatenate(rows + [spare_rows(points)], axis=0).T


def source_side(points):
    tail = tail_rows(neg_norm_parts(points.astype(jnp.float32)), 0, 3, TAIL)
    return jnp.concatenate(
        [points, points, points, tail.astype(jnp.bfloat16), spare_rows(points)], axis=0
    )


def tile_term(target, points, weights):
    exponent = jnp.dot(target, source_side(points), preferred_element_type=jnp.float32)
    tile = jnp.exp2(exponent).astype(jnp.bfloat16)
    return lax.dot_general(
        tile, weights, (((1,), (1,)), ((), ())), preferred_element_type=jnp.float32
    )


def local_kernel(depth_count, far_scale, points_ref, weights_ref, nodes_ref, self_ref, far_ref):
    points = points_ref[...]
    target = target_side(points)
    self_ref[...] = tile_term(target, points, weights_ref[...]).T
    total = jnp.zeros((LEAF, RHS), jnp.float32)
    for level in range(depth_count):
        total = total + tile_term(target, nodes_ref[level, :D, :], nodes_ref[level, D:, :])
    far_ref[...] = total.T * far_scale


def near_kernel(leaves_dev, near_scale, owner_ref, place_ref, start_ref, points_ref, self_ref,
                blocks_ref, out_ref, held, sems):
    total_items = start_ref[leaves_dev]

    def fetch(item):
        slot = lax.rem(item, SLOTS)
        column = pl.multiple_of(place_ref[item] * LEAF, LEAF)
        return pltpu.make_async_copy(
            blocks_ref.at[owner_ref[item], :, pl.ds(column, LEAF)], held.at[slot], sems.at[slot]
        )

    for ahead in range(SLOTS - 1):
        @pl.when(ahead < total_items)
        def _():
            fetch(ahead).start()

    def leaf_step(leaf, carry):
        columns = pl.ds(pl.multiple_of(leaf * LEAF, LEAF), LEAF)
        target = target_side(points_ref[:, columns])

        def item_step(item, running):
            @pl.when(item + SLOTS - 1 < total_items)
            def _():
                fetch(item + SLOTS - 1).start()
            fetch(item).wait()
            slot = lax.rem(item, SLOTS)
            return running + tile_term(target, held[slot, :D, :], held[slot, D:, :])

        total = lax.fori_loop(
            start_ref[leaf], start_ref[leaf + 1], item_step, jnp.zeros((LEAF, RHS), jnp.float32)
        )
        out_ref[:, columns] = (total.T + self_ref[:, columns]) * near_scale
        return carry

    lax.fori_loop(0, leaves_dev, leaf_step, 0)


def merged(mine, sibling, upper_bit):
    half = SKEL // 2
    parts = []
    for node in (mine, sibling):
        weights = node[D:, :half].astype(jnp.float32) + node[D:, half:].astype(jnp.float32)
        parts.append(
            jnp.concatenate([node[:D, :half].astype(jnp.float32), weights], axis=0)
        )
    lower = jnp.where(upper_bit == 0, parts[0], parts[1])
    upper = jnp.where(upper_bit == 0, parts[1], parts[0])
    return jnp.concatenate([lower, upper], axis=1).astype(jnp.bfloat16)


def layer_kernel(n_dev, near_scale, far_scale, item_ref, spot_ref, leaves_ref, base_ref,
                 near_ref, far_ref, below1, above1, below2, above2, below3, above3, points,
                 targets, results, outbox, inbox, mine, sibling, line_recv, line_send,
                 point_send, point_recv, sum_send, sum_recv, node_send, node_recv):
    planes = n_dev // 8
    depth_count = n_dev.bit_length() - 1
    leaves_dev = leaves_ref.shape[0]
    half = leaves_dev // 2
    held = (leaves_ref, below1, above1, below2, above2, below3, above3)
    me = lax.axis_index("leaf")
    bits = [(me // 2**level) % 2 for level in range(depth_count)]
    partners = [me + (1 - 2 * bits[level]) * 2**level for level in range(depth_count)]
    plane = me // 8

    def peer(apart):
        found = me
        for level in range(3):
            found = found + (1 - 2 * bits[level]) * 2**level * (apart // 2**level % 2)
        return found

    def remote(source, target, send_sem, recv_sem, device):
        return pltpu.make_async_remote_copy(
            src_ref=source, dst_ref=target, send_sem=send_sem, recv_sem=recv_sem,
            device_id=(device,), device_id_type=pl.DeviceIdType.MESH,
        )

    barrier = pltpu.get_barrier_semaphore()

    def greet(device):
        pl.semaphore_signal(
            barrier, inc=1, device_id=(device,), device_id_type=pl.DeviceIdType.MESH
        )

    for device in [peer(apart) for apart in range(1, 8)] + partners[4:]:
        greet(device)

    @pl.when(plane < planes - 1)
    def _():
        greet(me + 8)

    @pl.when(plane > 0)
    def _():
        greet(me - 8)

    pl.semaphore_wait(
        barrier,
        7 + len(partners[4:]) + jnp.where(plane < planes - 1, 1, 0) + jnp.where(plane > 0, 1, 0),
    )

    def line_copy(step, above, part):
        target = 2 * step - 1 + above
        source = 0 if step == 1 else target - 2
        piece = pl.ds(part * half, half)
        return remote(
            held[source].at[piece], held[target].at[piece], line_send.at[target - 1, part],
            line_recv.at[target - 1, part], me - 8 if above else me + 8,
        )

    def sends(step, above):
        if above:
            return (plane > 0) & (plane + step - 1 < planes)
        return (plane < planes - 1) & (plane - step + 1 >= 0)

    def receives(step, above):
        return plane + step < planes if above else plane - step >= 0

    def line_step(step):
        for part in range(2):
            for above in range(2):
                @pl.when(receives(step, above))
                def _():
                    line_copy(step, above, part).wait_recv()
                if step + 1 < planes:
                    @pl.when(sends(step + 1, above))
                    def _():
                        line_copy(step + 1, above, part).start()

    def point_copy(apart, part=None):
        if apart in (1, 2, 4):
            source, over = leaves_ref.at[:, pl.ds(0, D)], apart
        elif apart == 6:
            source, over = points.at[2 + 2 * part], 4 - 2 * part
        else:
            source, over = points.at[apart - 1], 1
        target = points.at[apart]
        if part is not None:
            source, target = source.at[pl.ds(part * half, half)], target.at[pl.ds(part * half, half)]
        slot = 0 if part is None else part
        return remote(
            source, target, point_send.at[apart, slot], point_recv.at[apart, slot], peer(over)
        )

    def relay_sides():
        for apart, part in ((2, 0), (4, 1)):
            point_copy(apart).wait_recv()
            point_copy(6, part).start()
            point_copy(apart + 1).start()

    def relay_across():
        for part in range(2):
            point_copy(6, part).wait_recv()
        point_copy(7).start()

    def sum_copy(apart):
        return remote(
            outbox.at[apart], inbox.at[apart], sum_send.at[apart], sum_recv.at[apart], peer(apart)
        )

    def node_copy(level):
        return remote(
            mine.at[level], sibling.at[level], node_send.at[level], node_recv.at[level],
            partners[level],
        )

    def columns(leaf):
        return pl.ds(pl.multiple_of(leaf * LEAF, LEAF), LEAF)

    def self_leaf(leaf, carry):
        target = target_side(leaves_ref[leaf, :D, :])
        targets[leaf] = target
        near_ref[:, columns(leaf)] = tile_term(
            target, leaves_ref[leaf, :D, :], leaves_ref[leaf, D:, :]
        ).T
        far_ref[:, columns(leaf)] = jnp.zeros((RHS, LEAF), jnp.float32)
        return carry

    def far_levels(first, last):
        def item(leaf, carry):
            target = targets[leaf]
            term = jnp.zeros((LEAF, RHS), jnp.float32)
            for level in range(first, last):
                term = term + tile_term(target, sibling[level, :D, :], sibling[level, D:, :])
            far_ref[:, columns(leaf)] += term.T
            return carry
        lax.fori_loop(0, leaves_dev, item, 0)

    def next_node(level):
        node_copy(level).wait_recv()
        if level + 1 < depth_count:
            mine[level + 1] = merged(mine[level], sibling[level], bits[level])
            node_copy(level + 1).start()

    def prepare(apart, carry):
        def one_leaf(leaf, inner):
            targets[apart * leaves_dev + leaf] = target_side(points[apart, leaf])
            return inner
        return lax.fori_loop(0, leaves_dev, one_leaf, carry)

    def finish(apart):
        def leaf_sum(leaf):
            first = (apart * leaves_dev + leaf) * NEAR
            total = results[spot_ref[first]]
            for slot in range(1, NEAR):
                total = total + results[spot_ref[first + slot]]
            return total

        @pl.when(apart == 0)
        def _():
            def own_leaf(leaf, carry):
                near_ref[:, columns(leaf)] += leaf_sum(leaf)
                return carry
            lax.fori_loop(0, leaves_dev, own_leaf, 0)

        @pl.when(apart > 0)
        def _():
            def peer_leaf(leaf, carry):
                outbox[apart, :, columns(leaf)] = leaf_sum(leaf).astype(jnp.bfloat16)
                return carry
            lax.fori_loop(0, leaves_dev, peer_leaf, 0)
            sum_copy(apart).start()

    def near_group(group, is_last):
        def readers(index, carry):
            apart = 7 - index

            first = (group * 8 + apart) * PER_PAIR
            total = jnp.zeros((LEAF, PER_PAIR * RHS), jnp.float32)
            for rank in range(PER_PAIR):
                block = held[group][item_ref[1, first + rank]]
                target = targets[apart * leaves_dev + item_ref[0, first + rank]]
                weights = [jnp.zeros((RHS, LEAF), jnp.bfloat16)] * PER_PAIR
                weights[rank] = block[D:]
                total = total + tile_term(target, block[:D], jnp.concatenate(weights, axis=0))
            results[pl.ds(first, PER_PAIR)] = total.T.reshape(PER_PAIR, RHS, LEAF)
            if is_last is not None:
                @pl.when(is_last)
                def _():
                    finish(apart)
            return carry
        lax.fori_loop(0, 7 if group == 0 else 8, readers, 0)

    def line_groups(step):
        for above in range(2):
            @pl.when(receives(step, above))
            def _():
                last = None
                if step >= planes // 2:
                    farther = plane < planes - 1 - plane
                    reach = jnp.where(farther, planes - 1 - plane, plane)
                    side = jnp.where(farther, 1, 0)
                    last = (reach == step) & (side == above)
                near_group(2 * step - 1 + above, last)

    for part in range(2):
        for above in range(2):
            @pl.when(sends(1, above))
            def _():
                line_copy(1, above, part).start()
    mine[0] = base_ref[...]
    node_copy(0).start()
    for apart in (1, 2, 4):
        point_copy(apart).start()
    results[7 * 8 * PER_PAIR] = jnp.zeros((RHS, LEAF), jnp.float32)
    lax.fori_loop(0, leaves_dev, self_leaf, 0)
    relay_sides()
    early = min(3, depth_count)
    for level in range(early):
        next_node(level)
    far_levels(0, early)
    line_step(1)
    relay_across()
    for level in range(early, depth_count):
        next_node(level)
    far_levels(early, depth_count)
    for apart in (1, 3, 5, 7):
        point_copy(apart).wait_recv()
    line_step(2)
    lax.fori_loop(1, 8, prepare, 0)
    near_group(0, None)
    for step in range(2, planes):
        if step > 2:
            line_step(step)
        line_groups(step - 1)
    line_groups(planes - 1)

    for apart in range(1, 8):
        sum_copy(apart).wait_recv()

    def scale(leaf, carry):
        total = near_ref[:, columns(leaf)]
        for apart in range(1, 8):
            total = total + inbox[apart, :, columns(leaf)].astype(jnp.float32)
        near_ref[:, columns(leaf)] = total * near_scale
        far_ref[:, columns(leaf)] = far_ref[:, columns(leaf)] * far_scale
        return carry
    lax.fori_loop(0, leaves_dev, scale, 0)

    for level in range(depth_count):
        node_copy(level).wait_send()
    for apart in range(1, 8):
        if apart == 6:
            point_copy(6, 0).wait_send()
            point_copy(6, 1).wait_send()
        else:
            point_copy(apart).wait_send()
        sum_copy(apart).wait_send()
    for step in range(1, planes):
        for part in range(2):
            for above in range(2):
                @pl.when(sends(step, above))
                def _():
                    line_copy(step, above, part).wait_send()


def fused(leaf_blocks, base_node, near_leaf, near_count, n_dev, my_index):
    leaves_dev = leaf_blocks.shape[0]
    p_dev = leaves_dev * LEAF
    slot_count = leaves_dev * NEAR
    depth_count = n_dev.bit_length() - 1
    planes = n_dev // 8
    spots = 7 * 8 * PER_PAIR

    readers = my_index ^ jnp.arange(8, dtype=jnp.int32)
    leaf_ids = near_leaf.reshape(n_dev, slot_count)[readers]
    counts = near_count.reshape(n_dev, leaves_dev)[readers]
    slot = jnp.arange(slot_count, dtype=jnp.int32)
    owner = leaf_ids // leaves_dev
    live = slot % NEAR < jnp.repeat(counts, NEAR, axis=1)
    live = live & (owner % 8 == my_index % 8)
    apart = owner // 8 - my_index // 8
    group = jnp.where(apart == 0, 0, 2 * jnp.abs(apart) - jnp.where(apart < 0, 1, 0))
    earlier = (slot[None, :] < slot[:, None])[None] & live[:, None, :]
    earlier = earlier & (group[:, None, :] == group[:, :, None])
    rank = jnp.sum(earlier.astype(jnp.int32), axis=2)
    reader = jnp.arange(8, dtype=jnp.int32)[:, None]
    spot = jnp.where(live, (group * 8 + reader) * PER_PAIR + rank, spots).astype(jnp.int32)
    fields = (slot[None, :] // NEAR) * leaves_dev + leaf_ids % leaves_dev
    spot = spot.reshape(-1)
    chosen = spot[None, :] == jnp.arange(spots, dtype=jnp.int32)[:, None]
    packed = jnp.sum(jnp.where(chosen, fields.reshape(1, -1), 0), axis=1).astype(jnp.int32)
    items = jnp.stack([packed // leaves_dev, packed % leaves_dev])

    tiles = leaves_dev * (depth_count + 1) + planes * 8 * PER_PAIR
    whole = pl.BlockSpec(memory_space=pltpu.VMEM)
    scalars = pl.BlockSpec(memory_space=pltpu.SMEM)
    dma = pltpu.SemaphoreType.DMA
    block_buffer = pltpu.VMEM((leaves_dev, ROWS, LEAF), jnp.bfloat16)
    return pl.pallas_call(
        functools.partial(
            layer_kernel, n_dev, 4.0 / math.sqrt(LEAF * (NEAR + 1)),
            4.0 / math.sqrt(p_dev * n_dev),
        ),
        in_specs=[scalars, scalars, whole, whole],
        out_specs=[whole, whole],
        out_shape=[jax.ShapeDtypeStruct((RHS, p_dev), jnp.float32)] * 2,
        scratch_shapes=[
            *[block_buffer] * 6,
            pltpu.VMEM((8, leaves_dev, D, LEAF), jnp.bfloat16),
            pltpu.VMEM((8 * leaves_dev, LEAF, DEPTH), jnp.bfloat16),
            pltpu.VMEM((spots + 1, RHS, LEAF), jnp.float32),
            pltpu.VMEM((8, RHS, p_dev), jnp.bfloat16),
            pltpu.VMEM((8, RHS, p_dev), jnp.bfloat16),
            pltpu.VMEM((depth_count, ROWS, SKEL), jnp.bfloat16),
            pltpu.VMEM((depth_count, ROWS, SKEL), jnp.bfloat16),
            dma((6, 2)),
            dma((6, 2)),
            dma((8, 2)),
            dma((8, 2)),
            dma((8,)),
            dma((8,)),
            dma((depth_count,)),
            dma((depth_count,)),
        ],
        compiler_params=pltpu.CompilerParams(
            collective_id=0, has_side_effects=True, vmem_limit_bytes=60 * 2**20
        ),
        cost_estimate=pl.CostEstimate(
            flops=tiles * 2 * LEAF * LEAF * (DEPTH + 256),
            bytes_accessed=4 * 2**20,
            transcendentals=tiles * LEAF * LEAF,
        ),
        name="exchange_and_tiles",
    )(items, spot, leaf_blocks, base_node)


def fold_child(nodes):
    half = nodes.shape[-1] // 2
    folded = nodes[..., D:, :half].astype(jnp.float32) + nodes[..., D:, half:].astype(jnp.float32)
    return jnp.concatenate([nodes[..., :D, :half], folded.astype(jnp.bfloat16)], axis=-2)


def sibling_nodes(nodes, my_index, depth_count):
    found = []
    for level in range(depth_count):
        found.append(lax.dynamic_index_in_dim(nodes, (my_index >> level) ^ 1, 0, keepdims=False))
        if level + 1 < depth_count:
            child = fold_child(nodes)
            nodes = jnp.concatenate([child[0::2], child[1::2]], axis=-1)
    return jnp.stack(found)


def per_device(points, weights, skel_index, assign, near_leaf, near_count):
    n_dev = lax.axis_size("leaf")
    my_index = lax.axis_index("leaf")
    depth_count = n_dev.bit_length() - 1
    p_dev = points.shape[1]
    leaves_dev = p_dev // LEAF

    member = (assign[None, :] == jnp.arange(SKEL, dtype=jnp.int32)[:, None]).astype(jnp.bfloat16)
    base_weights = lax.dot_general(
        weights, member, (((1,), (1,)), ((), ())), preferred_element_type=jnp.float32
    )
    base_node = jnp.concatenate([points[:, skel_index], base_weights.astype(jnp.bfloat16)], axis=0)
    stacked = jnp.concatenate([points, weights], axis=0)
    if n_dev == 32 and PER_PAIR * (n_dev - 1) >= leaves_dev * NEAR:
        leaf_blocks = stacked.reshape(ROWS, leaves_dev, LEAF).transpose(1, 0, 2)
        return fused(leaf_blocks, base_node, near_leaf, near_count, n_dev, my_index)
    base_node, stacked = lax.optimization_barrier((base_node, stacked))
    nodes = lax.all_gather(base_node, "leaf")
    blocks = lax.all_gather(stacked, "leaf")

    slot_count = leaves_dev * NEAR
    my_leaf = lax.dynamic_slice_in_dim(near_leaf, my_index * leaves_dev, leaves_dev).reshape(-1)
    my_count = lax.dynamic_slice_in_dim(near_count, my_index * leaves_dev, leaves_dev)
    before = jnp.arange(leaves_dev + 1)[:, None] > jnp.arange(leaves_dev)[None, :]
    start = jnp.sum(jnp.where(before, my_count[None, :], 0), axis=1).astype(jnp.int32)
    slot = jnp.arange(slot_count, dtype=jnp.int32)
    live = slot % NEAR < jnp.repeat(my_count, NEAR)
    spot = jnp.where(live, jnp.repeat(start[:-1], NEAR) + slot % NEAR, slot_count)
    chosen = spot[None, :] == slot[:, None]
    item_leaf = jnp.sum(jnp.where(chosen, my_leaf[None, :], 0), axis=1).astype(jnp.int32)

    siblings = sibling_nodes(nodes, my_index, depth_count)
    tile_flops = 2 * LEAF * LEAF * (DEPTH + 256)
    column_block = lambda rows: pl.BlockSpec((rows, LEAF), lambda leaf: (0, leaf))
    self_term, far_field = pl.pallas_call(
        functools.partial(local_kernel, depth_count, 4.0 / math.sqrt(p_dev * n_dev)),
        grid=(leaves_dev,),
        in_specs=[
            column_block(D),
            column_block(RHS),
            pl.BlockSpec((depth_count, ROWS, SKEL), lambda leaf: (0, 0, 0)),
        ],
        out_specs=[column_block(RHS), column_block(RHS)],
        out_shape=[jax.ShapeDtypeStruct((RHS, p_dev), jnp.float32)] * 2,
        compiler_params=pltpu.CompilerParams(vmem_limit_bytes=48 * 2**20),
        cost_estimate=pl.CostEstimate(
            flops=leaves_dev * (depth_count + 1) * tile_flops,
            bytes_accessed=4 * 2**20,
            transcendentals=leaves_dev * (depth_count + 1) * LEAF * LEAF,
        ),
        name="local_and_far",
    )(points, weights, siblings)

    whole = pl.BlockSpec(memory_space=pltpu.VMEM)
    scalars = pl.BlockSpec(memory_space=pltpu.SMEM)
    near_field = pl.pallas_call(
        functools.partial(near_kernel, leaves_dev, 4.0 / math.sqrt(LEAF * (NEAR + 1))),
        in_specs=[scalars, scalars, scalars, whole, whole, pl.BlockSpec(memory_space=pl.ANY)],
        out_specs=whole,
        out_shape=jax.ShapeDtypeStruct((RHS, p_dev), jnp.float32),
        scratch_shapes=[
            pltpu.VMEM((SLOTS, ROWS, LEAF), jnp.bfloat16),
            pltpu.SemaphoreType.DMA((SLOTS,)),
        ],
        compiler_params=pltpu.CompilerParams(vmem_limit_bytes=48 * 2**20),
        cost_estimate=pl.CostEstimate(
            flops=slot_count * tile_flops,
            bytes_accessed=slot_count * ROWS * LEAF * 2,
            transcendentals=slot_count * LEAF * LEAF,
        ),
        name="near_blocks",
    )(item_leaf // leaves_dev, item_leaf % leaves_dev, start, points, self_term, blocks)
    return (near_field, far_field)


def solution(mesh):
    return jax.shard_map(
        per_device,
        mesh=mesh,
        in_specs=(P(None, "leaf"), P(None, "leaf"), P("leaf"), P("leaf"), P(), P()),
        out_specs=(P(None, "leaf"), P(None, "leaf")),
        check_vma=False,
    )
```

```python
import functools
import math

import jax
import jax.numpy as jnp
from jax import lax
from jax.experimental import pallas as pl
from jax.experimental.pallas import tpu as pltpu
from jax.sharding import PartitionSpec as P

D = 64
RHS = 32
LEAF = 512
SKEL = 512
NEAR = 12
ROWS = D + RHS
DEPTH = 256
SCALE2 = 1.0 / (D * math.log(2.0))
SLOTS = 4
TAIL = 16
PARTS = 4
PER_PAIR = 4


def three_parts(x):
    high = x.astype(jnp.bfloat16).astype(jnp.float32)
    rest = x - high
    mid = rest.astype(jnp.bfloat16).astype(jnp.float32)
    low = (rest - mid).astype(jnp.bfloat16).astype(jnp.float32)
    return high, mid, low


def neg_norm_parts(points32):
    norm = jnp.sum(points32 * points32, axis=0, keepdims=True) * (-SCALE2)
    return three_parts(norm)


def tail_rows(parts, first, ones_first, rows):
    row = lax.broadcasted_iota(jnp.int32, (rows, parts[0].shape[1]), 0)
    tail = jnp.where((row >= ones_first) & (row < ones_first + 3), 1.0, 0.0)
    for step, part in enumerate(parts):
        tail = jnp.where(row == first + step, part, tail)
    return tail


def spare_rows(points):
    return jnp.zeros((DEPTH - 3 * D - TAIL, points.shape[1]), jnp.bfloat16)


def target_side(points):
    points32 = points.astype(jnp.float32)
    parts = three_parts(points32 * (2.0 * SCALE2))
    tail = tail_rows(neg_norm_parts(points32), 3, 0, TAIL)
    rows = [part.astype(jnp.bfloat16) for part in (*parts, tail)]
    return jnp.concatenate(rows + [spare_rows(points)], axis=0).T


def source_side(points):
    tail = tail_rows(neg_norm_parts(points.astype(jnp.float32)), 0, 3, TAIL)
    return jnp.concatenate(
        [points, points, points, tail.astype(jnp.bfloat16), spare_rows(points)], axis=0
    )


def tile_term(target, points, weights):
    exponent = jnp.dot(target, source_side(points), preferred_element_type=jnp.float32)
    tile = jnp.exp2(exponent).astype(jnp.bfloat16)
    return lax.dot_general(
        tile, weights, (((1,), (1,)), ((), ())), preferred_element_type=jnp.float32
    )


def local_kernel(depth_count, far_scale, points_ref, weights_ref, nodes_ref, self_ref, far_ref):
    points = points_ref[...]
    target = target_side(points)
    self_ref[...] = tile_term(target, points, weights_ref[...]).T
    total = jnp.zeros((LEAF, RHS), jnp.float32)
    for level in range(depth_count):
        total = total + tile_term(target, nodes_ref[level, :D, :], nodes_ref[level, D:, :])
    far_ref[...] = total.T * far_scale


def near_kernel(leaves_dev, near_scale, owner_ref, place_ref, start_ref, points_ref, self_ref,
                blocks_ref, out_ref, held, sems):
    total_items = start_ref[leaves_dev]

    def fetch(item):
        slot = lax.rem(item, SLOTS)
        column = pl.multiple_of(place_ref[item] * LEAF, LEAF)
        return pltpu.make_async_copy(
            blocks_ref.at[owner_ref[item], :, pl.ds(column, LEAF)], held.at[slot], sems.at[slot]
        )

    for ahead in range(SLOTS - 1):
        @pl.when(ahead < total_items)
        def _():
            fetch(ahead).start()

    def leaf_step(leaf, carry):
        columns = pl.ds(pl.multiple_of(leaf * LEAF, LEAF), LEAF)
        target = target_side(points_ref[:, columns])

        def item_step(item, running):
            @pl.when(item + SLOTS - 1 < total_items)
            def _():
                fetch(item + SLOTS - 1).start()
            fetch(item).wait()
            slot = lax.rem(item, SLOTS)
            return running + tile_term(target, held[slot, :D, :], held[slot, D:, :])

        total = lax.fori_loop(
            start_ref[leaf], start_ref[leaf + 1], item_step, jnp.zeros((LEAF, RHS), jnp.float32)
        )
        out_ref[:, columns] = (total.T + self_ref[:, columns]) * near_scale
        return carry

    lax.fori_loop(0, leaves_dev, leaf_step, 0)


def merged(mine, sibling, upper_bit):
    half = SKEL // 2
    parts = []
    for node in (mine, sibling):
        weights = node[D:, :half].astype(jnp.float32) + node[D:, half:].astype(jnp.float32)
        parts.append(
            jnp.concatenate([node[:D, :half].astype(jnp.float32), weights], axis=0)
        )
    lower = jnp.where(upper_bit == 0, parts[0], parts[1])
    upper = jnp.where(upper_bit == 0, parts[1], parts[0])
    return jnp.concatenate([lower, upper], axis=1).astype(jnp.bfloat16)


def layer_kernel(n_dev, near_scale, far_scale, item_ref, spot_ref, leaves_ref, base_ref,
                 near_ref, far_ref, below1, above1, below2, above2, below3, above3, points,
                 targets, results, outbox, inbox, mine, sibling, line_recv, line_send,
                 point_send, point_recv, sum_send, sum_recv, node_send, node_recv):
    planes = n_dev // 8
    depth_count = n_dev.bit_length() - 1
    leaves_dev = leaves_ref.shape[0]
    half, share = leaves_dev // 2, leaves_dev // PARTS
    held = (leaves_ref, below1, above1, below2, above2, below3, above3)
    me = lax.axis_index("leaf")
    bits = [(me // 2**level) % 2 for level in range(depth_count)]
    partners = [me + (1 - 2 * bits[level]) * 2**level for level in range(depth_count)]
    plane = me // 8

    def peer(apart):
        found = me
        for level in range(3):
            found = found + (1 - 2 * bits[level]) * 2**level * (apart // 2**level % 2)
        return found

    def remote(source, target, send_sem, recv_sem, device):
        return pltpu.make_async_remote_copy(
            src_ref=source, dst_ref=target, send_sem=send_sem, recv_sem=recv_sem,
            device_id=(device,), device_id_type=pl.DeviceIdType.MESH,
        )

    barrier = pltpu.get_barrier_semaphore()

    def greet(device):
        pl.semaphore_signal(
            barrier, inc=1, device_id=(device,), device_id_type=pl.DeviceIdType.MESH
        )

    for device in [peer(apart) for apart in range(1, 8)] + partners[4:]:
        greet(device)

    @pl.when(plane < planes - 1)
    def _():
        greet(me + 8)

    @pl.when(plane > 0)
    def _():
        greet(me - 8)

    pl.semaphore_wait(
        barrier,
        7 + len(partners[4:]) + jnp.where(plane < planes - 1, 1, 0) + jnp.where(plane > 0, 1, 0),
    )

    def line_copy(step, above, part):
        target = 2 * step - 1 + above
        source = 0 if step == 1 else target - 2
        piece = pl.ds(part * share, share)
        return remote(
            held[source].at[piece], held[target].at[piece], line_send.at[target - 1, part],
            line_recv.at[target - 1, part], me - 8 if above else me + 8,
        )

    def sends(step, above):
        if above:
            return (plane > 0) & (plane + step - 1 < planes)
        return (plane < planes - 1) & (plane - step + 1 >= 0)

    def receives(step, above):
        return plane + step < planes if above else plane - step >= 0

    def line_step(step):
        for part in range(PARTS):
            for above in range(2):
                @pl.when(receives(step, above))
                def _():
                    line_copy(step, above, part).wait_recv()
                if step + 1 < planes:
                    @pl.when(sends(step + 1, above))
                    def _():
                        line_copy(step + 1, above, part).start()

    def point_copy(apart, part=None):
        if apart in (1, 2, 4):
            source, over = leaves_ref.at[:, pl.ds(0, D)], apart
        elif apart == 6:
            source, over = points.at[2 + 2 * part], 4 - 2 * part
        else:
            source, over = points.at[apart - 1], 1
        target = points.at[apart]
        if part is not None:
            source, target = source.at[pl.ds(part * half, half)], target.at[pl.ds(part * half, half)]
        slot = 0 if part is None else part
        return remote(
            source, target, point_send.at[apart, slot], point_recv.at[apart, slot], peer(over)
        )

    def relay_sides():
        for apart, part in ((2, 0), (4, 1)):
            point_copy(apart).wait_recv()
            point_copy(6, part).start()
            point_copy(apart + 1).start()

    def relay_across():
        for part in range(2):
            point_copy(6, part).wait_recv()
        point_copy(7).start()

    def sum_copy(apart):
        return remote(
            outbox.at[apart], inbox.at[apart], sum_send.at[apart], sum_recv.at[apart], peer(apart)
        )

    def node_copy(level):
        return remote(
            mine.at[level], sibling.at[level], node_send.at[level], node_recv.at[level],
            partners[level],
        )

    def columns(leaf):
        return pl.ds(pl.multiple_of(leaf * LEAF, LEAF), LEAF)

    def self_leaf(leaf, carry):
        target = target_side(leaves_ref[leaf, :D, :])
        targets[leaf] = target
        near_ref[:, columns(leaf)] = tile_term(
            target, leaves_ref[leaf, :D, :], leaves_ref[leaf, D:, :]
        ).T
        far_ref[:, columns(leaf)] = jnp.zeros((RHS, LEAF), jnp.float32)
        return carry

    def far_levels(first, last):
        def item(leaf, carry):
            target = targets[leaf]
            term = jnp.zeros((LEAF, RHS), jnp.float32)
            for level in range(first, last):
                term = term + tile_term(target, sibling[level, :D, :], sibling[level, D:, :])
            far_ref[:, columns(leaf)] += term.T
            return carry
        lax.fori_loop(0, leaves_dev, item, 0)

    def next_node(level):
        node_copy(level).wait_recv()
        if level + 1 < depth_count:
            mine[level + 1] = merged(mine[level], sibling[level], bits[level])
            node_copy(level + 1).start()

    def prepare(apart, carry):
        def one_leaf(leaf, inner):
            targets[apart * leaves_dev + leaf] = target_side(points[apart, leaf])
            return inner
        return lax.fori_loop(0, leaves_dev, one_leaf, carry)

    def finish(apart):
        def leaf_sum(leaf):
            first = (apart * leaves_dev + leaf) * NEAR
            total = results[spot_ref[first]]
            for slot in range(1, NEAR):
                total = total + results[spot_ref[first + slot]]
            return total

        @pl.when(apart == 0)
        def _():
            def own_leaf(leaf, carry):
                near_ref[:, columns(leaf)] += leaf_sum(leaf)
                return carry
            lax.fori_loop(0, leaves_dev, own_leaf, 0)

        @pl.when(apart > 0)
        def _():
            def peer_leaf(leaf, carry):
                outbox[apart, :, columns(leaf)] = leaf_sum(leaf).astype(jnp.bfloat16)
                return carry
            lax.fori_loop(0, leaves_dev, peer_leaf, 0)
            sum_copy(apart).start()

    def near_group(group, is_last):
        def readers(index, carry):
            apart = 7 - index

            first = (group * 8 + apart) * PER_PAIR
            total = jnp.zeros((LEAF, PER_PAIR * RHS), jnp.float32)
            for rank in range(PER_PAIR):
                block = held[group][item_ref[1, first + rank]]
                target = targets[apart * leaves_dev + item_ref[0, first + rank]]
                weights = [jnp.zeros((RHS, LEAF), jnp.bfloat16)] * PER_PAIR
                weights[rank] = block[D:]
                total = total + tile_term(target, block[:D], jnp.concatenate(weights, axis=0))
            results[pl.ds(first, PER_PAIR)] = total.T.reshape(PER_PAIR, RHS, LEAF)
            if is_last is not None:
                @pl.when(is_last)
                def _():
                    finish(apart)
            return carry
        lax.fori_loop(0, 7 if group == 0 else 8, readers, 0)

    def line_groups(step):
        for above in range(2):
            @pl.when(receives(step, above))
            def _():
                last = None
                if step >= planes // 2:
                    farther = plane < planes - 1 - plane
                    reach = jnp.where(farther, planes - 1 - plane, plane)
                    side = jnp.where(farther, 1, 0)
                    last = (reach == step) & (side == above)
                near_group(2 * step - 1 + above, last)

    for part in range(PARTS):
        for above in range(2):
            @pl.when(sends(1, above))
            def _():
                line_copy(1, above, part).start()
    mine[0] = base_ref[...]
    node_copy(0).start()
    for apart in (1, 2, 4):
        point_copy(apart).start()
    results[7 * 8 * PER_PAIR] = jnp.zeros((RHS, LEAF), jnp.float32)
    lax.fori_loop(0, leaves_dev, self_leaf, 0)
    relay_sides()
    early = min(3, depth_count)
    for level in range(early):
        next_node(level)
    far_levels(0, early)
    line_step(1)
    relay_across()
    for apart in (1, 3, 5, 7):
        point_copy(apart).wait_recv()
    lax.fori_loop(1, 8, prepare, 0)
    line_step(2)
    for level in range(early, depth_count - 1):
        next_node(level)
    near_group(0, None)
    line_groups(1)
    next_node(depth_count - 1)
    far_levels(early, depth_count)
    line_groups(2)
    for step in range(3, planes):
        line_step(step)
        line_groups(step)

    for apart in range(1, 8):
        sum_copy(apart).wait_recv()

    def scale(leaf, carry):
        total = near_ref[:, columns(leaf)]
        for apart in range(1, 8):
            total = total + inbox[apart, :, columns(leaf)].astype(jnp.float32)
        near_ref[:, columns(leaf)] = total * near_scale
        far_ref[:, columns(leaf)] = far_ref[:, columns(leaf)] * far_scale
        return carry
    lax.fori_loop(0, leaves_dev, scale, 0)

    for level in range(depth_count):
        node_copy(level).wait_send()
    for apart in range(1, 8):
        if apart == 6:
            point_copy(6, 0).wait_send()
            point_copy(6, 1).wait_send()
        else:
            point_copy(apart).wait_send()
        sum_copy(apart).wait_send()
    for step in range(1, planes):
        for part in range(PARTS):
            for above in range(2):
                @pl.when(sends(step, above))
                def _():
                    line_copy(step, above, part).wait_send()


def fused(leaf_blocks, base_node, near_leaf, near_count, n_dev, my_index):
    leaves_dev = leaf_blocks.shape[0]
    p_dev = leaves_dev * LEAF
    slot_count = leaves_dev * NEAR
    depth_count = n_dev.bit_length() - 1
    planes = n_dev // 8
    spots = 7 * 8 * PER_PAIR

    readers = my_index ^ jnp.arange(8, dtype=jnp.int32)
    leaf_ids = near_leaf.reshape(n_dev, slot_count)[readers]
    counts = near_count.reshape(n_dev, leaves_dev)[readers]
    slot = jnp.arange(slot_count, dtype=jnp.int32)
    owner = leaf_ids // leaves_dev
    live = slot % NEAR < jnp.repeat(counts, NEAR, axis=1)
    live = live & (owner % 8 == my_index % 8)
    apart = owner // 8 - my_index // 8
    group = jnp.where(apart == 0, 0, 2 * jnp.abs(apart) - jnp.where(apart < 0, 1, 0))
    earlier = (slot[None, :] < slot[:, None])[None] & live[:, None, :]
    earlier = earlier & (group[:, None, :] == group[:, :, None])
    rank = jnp.sum(earlier.astype(jnp.int32), axis=2)
    reader = jnp.arange(8, dtype=jnp.int32)[:, None]
    spot = jnp.where(live, (group * 8 + reader) * PER_PAIR + rank, spots).astype(jnp.int32)
    fields = (slot[None, :] // NEAR) * leaves_dev + leaf_ids % leaves_dev
    spot = spot.reshape(-1)
    chosen = spot[None, :] == jnp.arange(spots, dtype=jnp.int32)[:, None]
    packed = jnp.sum(jnp.where(chosen, fields.reshape(1, -1), 0), axis=1).astype(jnp.int32)
    items = jnp.stack([packed // leaves_dev, packed % leaves_dev])

    tiles = leaves_dev * (depth_count + 1) + planes * 8 * PER_PAIR
    whole = pl.BlockSpec(memory_space=pltpu.VMEM)
    scalars = pl.BlockSpec(memory_space=pltpu.SMEM)
    dma = pltpu.SemaphoreType.DMA
    block_buffer = pltpu.VMEM((leaves_dev, ROWS, LEAF), jnp.bfloat16)
    return pl.pallas_call(
        functools.partial(
            layer_kernel, n_dev, 4.0 / math.sqrt(LEAF * (NEAR + 1)),
            4.0 / math.sqrt(p_dev * n_dev),
        ),
        in_specs=[scalars, scalars, whole, whole],
        out_specs=[whole, whole],
        out_shape=[jax.ShapeDtypeStruct((RHS, p_dev), jnp.float32)] * 2,
        scratch_shapes=[
            *[block_buffer] * 6,
            pltpu.VMEM((8, leaves_dev, D, LEAF), jnp.bfloat16),
            pltpu.VMEM((8 * leaves_dev, LEAF, DEPTH), jnp.bfloat16),
            pltpu.VMEM((spots + 1, RHS, LEAF), jnp.float32),
            pltpu.VMEM((8, RHS, p_dev), jnp.bfloat16),
            pltpu.VMEM((8, RHS, p_dev), jnp.bfloat16),
            pltpu.VMEM((depth_count, ROWS, SKEL), jnp.bfloat16),
            pltpu.VMEM((depth_count, ROWS, SKEL), jnp.bfloat16),
            dma((6, PARTS)),
            dma((6, PARTS)),
            dma((8, 2)),
            dma((8, 2)),
            dma((8,)),
            dma((8,)),
            dma((depth_count,)),
            dma((depth_count,)),
        ],
        compiler_params=pltpu.CompilerParams(
            collective_id=0, has_side_effects=True, vmem_limit_bytes=60 * 2**20
        ),
        cost_estimate=pl.CostEstimate(
            flops=tiles * 2 * LEAF * LEAF * (DEPTH + 256),
            bytes_accessed=4 * 2**20,
            transcendentals=tiles * LEAF * LEAF,
        ),
        name="exchange_and_tiles",
    )(items, spot, leaf_blocks, base_node)


def fold_child(nodes):
    half = nodes.shape[-1] // 2
    folded = nodes[..., D:, :half].astype(jnp.float32) + nodes[..., D:, half:].astype(jnp.float32)
    return jnp.concatenate([nodes[..., :D, :half], folded.astype(jnp.bfloat16)], axis=-2)


def sibling_nodes(nodes, my_index, depth_count):
    found = []
    for level in range(depth_count):
        found.append(lax.dynamic_index_in_dim(nodes, (my_index >> level) ^ 1, 0, keepdims=False))
        if level + 1 < depth_count:
            child = fold_child(nodes)
            nodes = jnp.concatenate([child[0::2], child[1::2]], axis=-1)
    return jnp.stack(found)


def per_device(points, weights, skel_index, assign, near_leaf, near_count):
    n_dev = lax.axis_size("leaf")
    my_index = lax.axis_index("leaf")
    depth_count = n_dev.bit_length() - 1
    p_dev = points.shape[1]
    leaves_dev = p_dev // LEAF

    member = (assign[None, :] == jnp.arange(SKEL, dtype=jnp.int32)[:, None]).astype(jnp.bfloat16)
    base_weights = lax.dot_general(
        weights, member, (((1,), (1,)), ((), ())), preferred_element_type=jnp.float32
    )
    base_node = jnp.concatenate([points[:, skel_index], base_weights.astype(jnp.bfloat16)], axis=0)
    stacked = jnp.concatenate([points, weights], axis=0)
    if n_dev == 32 and PER_PAIR * (n_dev - 1) >= leaves_dev * NEAR:
        leaf_blocks = stacked.reshape(ROWS, leaves_dev, LEAF).transpose(1, 0, 2)
        return fused(leaf_blocks, base_node, near_leaf, near_count, n_dev, my_index)
    base_node, stacked = lax.optimization_barrier((base_node, stacked))
    nodes = lax.all_gather(base_node, "leaf")
    blocks = lax.all_gather(stacked, "leaf")

    slot_count = leaves_dev * NEAR
    my_leaf = lax.dynamic_slice_in_dim(near_leaf, my_index * leaves_dev, leaves_dev).reshape(-1)
    my_count = lax.dynamic_slice_in_dim(near_count, my_index * leaves_dev, leaves_dev)
    before = jnp.arange(leaves_dev + 1)[:, None] > jnp.arange(leaves_dev)[None, :]
    start = jnp.sum(jnp.where(before, my_count[None, :], 0), axis=1).astype(jnp.int32)
    slot = jnp.arange(slot_count, dtype=jnp.int32)
    live = slot % NEAR < jnp.repeat(my_count, NEAR)
    spot = jnp.where(live, jnp.repeat(start[:-1], NEAR) + slot % NEAR, slot_count)
    chosen = spot[None, :] == slot[:, None]
    item_leaf = jnp.sum(jnp.where(chosen, my_leaf[None, :], 0), axis=1).astype(jnp.int32)

    siblings = sibling_nodes(nodes, my_index, depth_count)
    tile_flops = 2 * LEAF * LEAF * (DEPTH + 256)
    column_block = lambda rows: pl.BlockSpec((rows, LEAF), lambda leaf: (0, leaf))
    self_term, far_field = pl.pallas_call(
        functools.partial(local_kernel, depth_count, 4.0 / math.sqrt(p_dev * n_dev)),
        grid=(leaves_dev,),
        in_specs=[
            column_block(D),
            column_block(RHS),
            pl.BlockSpec((depth_count, ROWS, SKEL), lambda leaf: (0, 0, 0)),
        ],
        out_specs=[column_block(RHS), column_block(RHS)],
        out_shape=[jax.ShapeDtypeStruct((RHS, p_dev), jnp.float32)] * 2,
        compiler_params=pltpu.CompilerParams(vmem_limit_bytes=48 * 2**20),
        cost_estimate=pl.CostEstimate(
            flops=leaves_dev * (depth_count + 1) * tile_flops,
            bytes_accessed=4 * 2**20,
            transcendentals=leaves_dev * (depth_count + 1) * LEAF * LEAF,
        ),
        name="local_and_far",
    )(points, weights, siblings)

    whole = pl.BlockSpec(memory_space=pltpu.VMEM)
    scalars = pl.BlockSpec(memory_space=pltpu.SMEM)
    near_field = pl.pallas_call(
        functools.partial(near_kernel, leaves_dev, 4.0 / math.sqrt(LEAF * (NEAR + 1))),
        in_specs=[scalars, scalars, scalars, whole, whole, pl.BlockSpec(memory_space=pl.ANY)],
        out_specs=whole,
        out_shape=jax.ShapeDtypeStruct((RHS, p_dev), jnp.float32),
        scratch_shapes=[
            pltpu.VMEM((SLOTS, ROWS, LEAF), jnp.bfloat16),
            pltpu.SemaphoreType.DMA((SLOTS,)),
        ],
        compiler_params=pltpu.CompilerParams(vmem_limit_bytes=48 * 2**20),
        cost_estimate=pl.CostEstimate(
            flops=slot_count * tile_flops,
            bytes_accessed=slot_count * ROWS * LEAF * 2,
            transcendentals=slot_count * LEAF * LEAF,
        ),
        name="near_blocks",
    )(item_leaf // leaves_dev, item_leaf % leaves_dev, start, points, self_term, blocks)
    return (near_field, far_field)


def solution(mesh):
    return jax.shard_map(
        per_device,
        mesh=mesh,
        in_specs=(P(None, "leaf"), P(None, "leaf"), P("leaf"), P("leaf"), P(), P()),
        out_specs=(P(None, "leaf"), P(None, "leaf")),
        check_vma=False,
    )
```
